256 devices in a mesh: dp: 4 (over y_hi, core), expert: 64 (over x, z, y_lo).
Axes of the slice: x: 4, y: 4 (y_hi: 2, y_lo: 2; y = y_hi * 2 + y_lo), z: 8, core: 2. Of those that a mesh axis runs over, the one named last changes fastest.
Arguments:
- tokens: bfloat16 [32768, 2048], P(('dp', 'expert')), may hold values from -6 to 6
- cotangent: bfloat16 [32768, 2048], P(('dp', 'expert')), may hold values from -6 to 6
- routes: int32 [32768, 3], P(('dp', 'expert')), may hold values from 0 to 63, as said below
- slot_index: int32 [32768, 3], P(('dp', 'expert')), may hold values from 0 to 7, as said below
- route_weight: float32 [32768, 3], P(('dp', 'expert')), may hold values from 0.05 to 0.6
- swap_flags: int32 [64], replicated, may hold values from 0 to 1, as said below
- w_gate_up: bfloat16 [64, 2048, 1536], P('expert', 'dp'), may hold values from -0.125 to 0.125
- w_down: bfloat16 [64, 768, 2048], P('expert', 'dp'), may hold values from -0.21875 to 0.21875
Outputs:
- grad_tokens: float32 [32768, 2048], P(('dp', 'expert'))
- grad_weight: float32 [32768, 3], P(('dp', 'expert'))
- grad_gate_up: float32 [64, 2048, 1536], P('expert', 'dp')
- grad_down: float32 [64, 768, 2048], P('expert', 'dp')
The draws below stay inside these ranges and needn't reach their ends.
Inputs may be any that keep to these rules, and one draw needn't show every extreme that they name: `routes`: each token names 3 different experts. Within each aligned block of 128 tokens (the tokens of one device) no expert is named more than 8 times, and one expert, the same in every block, is named exactly 8 times in every block. `slot_index`: within each aligned block of 128 tokens, the assignments to one expert have distinct slots. swap_flags[e] equals swap_flags[e XOR (32)], and swap_flags[63] is 1.
All inputs are finite; a program needn't handle non-finite values.
Results may differ from the reference program's by a relative error of at most 0.011.
Values may be sent and summed in bfloat16 or wider, within the bound.
A program may use at most 128 MiB of HBM per device.

```python
import math
import jax
import jax.numpy as jnp
from jax import lax

D = 2048
FF = 768
TOK_DEV = 128
TOP = 3
EXPERTS = 64
TOKENS = 32768
CAP_SRC = 8
N_DP = 4


def route_table(key):
    hot = jax.random.randint(jax.random.fold_in(key, 11), (), 0, EXPERTS)
    blocks = TOKENS // TOK_DEV
    block_keys = jax.random.split(jax.random.fold_in(key, 12), blocks)

    def one_block(block_key):
        key_cold, key_noise, key_shift, key_order = jax.random.split(block_key, 4)
        expert_ids = jnp.arange(EXPERTS, dtype=jnp.int32)
        coldness = jnp.where(expert_ids == hot, 0, jax.random.randint(key_cold, (EXPERTS,), 1, 9))
        depth = jnp.arange(CAP_SRC, dtype=jnp.int32)
        noise = jax.random.randint(key_noise, (EXPERTS, CAP_SRC), 0, 64)
        score = depth[None, :] * coldness[:, None] * 64 + noise
        ranked = jnp.argsort(score.reshape(-1), stable=True)
        picked = jnp.sort(ranked[:TOK_DEV * TOP]).astype(jnp.int32)
        chosen = picked // CAP_SRC
        depth_of = picked % CAP_SRC
        shift = jax.random.randint(key_shift, (EXPERTS,), 0, CAP_SRC)
        slot_value = (depth_of + shift[chosen]) % CAP_SRC
        order_tok = jax.random.permutation(key_order, TOK_DEV)
        position = jnp.arange(TOK_DEV * TOP, dtype=jnp.int32)
        token = order_tok[position % TOK_DEV]
        column = position // TOK_DEV
        route_block = jnp.zeros((TOK_DEV, TOP), jnp.int32).at[token, column].set(chosen)
        slot_block = jnp.zeros((TOK_DEV, TOP), jnp.int32).at[token, column].set(slot_value)
        return (route_block, slot_block)
    route_all, slot_all = jax.vmap(one_block)(block_keys)
    return (route_all.reshape(TOKENS, TOP), slot_all.reshape(TOKENS, TOP))


def draw_routes(key, part):
    shared = route_table(key)
    return shared[0].astype(jnp.int32)


def draw_slot_index(key, part):
    shared = route_table(key)
    return shared[1].astype(jnp.int32)


def draw_swap_flags(key, part):
    key = jax.random.fold_in(key, 7)
    half_count = EXPERTS // 2
    flag_bits = jax.random.randint(key, (half_count,), 0, 2)
    flag_bits = jnp.where(jnp.arange(half_count) == half_count - 1, 1, flag_bits)
    return jnp.concatenate([flag_bits, flag_bits]).astype(jnp.int32)


def block_levels(stream_key, extent, cuts, smallest, largest):
    loudness = 1.0
    for dim, parts in cuts:
        steps = jax.random.uniform(jax.random.fold_in(jax.random.fold_in(stream_key, 6), dim), (parts,), jnp.float32, smallest / len(cuts), largest / len(cuts))
        loudness = loudness * jnp.repeat(jnp.exp(steps), extent[dim] // parts).reshape((-1,) + (1,) * (len(extent) - 1 - dim))
    return loudness


def gaussian(stream_key, dims, deviation, most, pieces=(), kind=jnp.bfloat16):
    result = deviation * jax.random.normal(stream_key, dims, jnp.float32)
    if pieces:
        result = result * block_levels(stream_key, dims, pieces, -0.22, 0.18)
    return jnp.clip(result, -most, most).astype(kind)


def setup_inputs(seed: int = 0) -> dict:
    key_list = jax.random.split(jax.random.key(seed), 9)
    tokens = gaussian(key_list[0], (TOKENS, D), 1.0, 6.0, ((0, 256),))
    cotangent = gaussian(key_list[1], (TOKENS, D), 1.0, 6.0, ((0, 256),))
    routes = draw_routes(jax.random.fold_in(key_list[8], 71), 0)
    slot_index = draw_slot_index(jax.random.fold_in(key_list[8], 71), 0)
    route_weight = jnp.clip(jnp.exp(math.log(0.6) - 2.4849067 * jax.random.uniform(key_list[4], (TOKENS, TOP), jnp.float32) ** block_levels(key_list[4], (TOKENS, TOP), ((0, 256),), -0.2, 0.2)), 0.05, 0.6)
    swap_flags = draw_swap_flags(jax.random.fold_in(key_list[8], 71), 0)
    w_gate_up = gaussian(key_list[6], (EXPERTS, D, 2 * FF), D ** -0.5, 0.125, ((0, 64), (1, 4)))
    w_down = gaussian(key_list[7], (EXPERTS, FF, D), FF ** -0.5, 0.21875, ((0, 64), (1, 4)))
    return {"tokens": tokens, "cotangent": cotangent, "routes": routes, "slot_index": slot_index, "route_weight": route_weight, "swap_flags": swap_flags, "w_gate_up": w_gate_up, "w_down": w_down}


def forward_pass(rows_in, gate_up_w, down_w):
    width = down_w.shape[0]
    gate_up = jnp.dot(rows_in, gate_up_w, preferred_element_type=jnp.float32)
    gate = gate_up[:, :width]
    up_val = gate_up[:, width:]
    sigmoid_gate = jax.nn.sigmoid(gate)
    silu_gate = gate * sigmoid_gate
    hidden_act = (silu_gate * up_val).astype(jnp.bfloat16)
    expert_out = jnp.dot(hidden_act, down_w, preferred_element_type=jnp.float32)
    return gate, up_val, sigmoid_gate, silu_gate, hidden_act, expert_out


def backward_pass(forward_vals, cot_in, weight_in, gate_up_w, down_w):
    gate, up_val, sigmoid_gate, silu_gate, hidden_act, expert_out = forward_vals
    prob_grad = jnp.sum(expert_out * cot_in.astype(jnp.float32), axis=1).astype(jnp.bfloat16)
    scaled = (weight_in.astype(jnp.float32)[:, None] * cot_in.astype(jnp.float32)).astype(jnp.bfloat16)
    hidden_grad = lax.dot_general(scaled, down_w, (((1,), (1,)), ((), ())), preferred_element_type=jnp.float32)
    gate_grad = (hidden_grad * up_val * sigmoid_gate * (1.0 + gate * (1.0 - sigmoid_gate))).astype(jnp.bfloat16)
    up_grad = (hidden_grad * silu_gate).astype(jnp.bfloat16)
    both_grad = jnp.concatenate([gate_grad, up_grad], axis=1)
    row_grad = lax.dot_general(both_grad, gate_up_w, (((1,), (1,)), ((), ())), preferred_element_type=jnp.float32).astype(jnp.bfloat16)
    return hidden_act, scaled, both_grad, row_grad, prob_grad


def reference(tokens, cotangent, routes, slot_index, route_weight, swap_flags, w_gate_up, w_down):
    blocks = TOKENS // TOK_DEV
    total_rows = blocks * CAP_SRC
    group_rows = total_rows // N_DP
    tok_ids = jnp.arange(TOKENS, dtype=jnp.int32)
    place = ((tok_ids // TOK_DEV)[:, None] * CAP_SRC + slot_index).astype(jnp.int32)
    table = jnp.full((EXPERTS, total_rows), TOKENS, jnp.int32).at[routes, place].set(jnp.broadcast_to(tok_ids[:, None], routes.shape))
    weight_table = jnp.zeros((EXPERTS, total_rows), jnp.bfloat16).at[routes, place].set(route_weight.astype(jnp.bfloat16))
    padded_tokens = jnp.concatenate([tokens, jnp.zeros((1, D), jnp.bfloat16)], axis=0)
    padded_cot = jnp.concatenate([cotangent, jnp.zeros((1, D), jnp.bfloat16)], axis=0)

    def one_expert(packed):
        index_row, weight_row, gate_up_w, down_w = packed
        rows_in = padded_tokens[index_row]
        cot_in = padded_cot[index_row]
        forward_vals = forward_pass(rows_in, gate_up_w, down_w)
        hidden_act, scaled, both_grad, row_grad, prob_grad = backward_pass(forward_vals, cot_in, weight_row, gate_up_w, down_w)
        part_gu = jnp.einsum("grd,grf->gdf", rows_in.astype(jnp.float32).reshape(N_DP, group_rows, D), both_grad.astype(jnp.float32).reshape(N_DP, group_rows, 2 * FF), precision=lax.Precision.HIGHEST)
        part_gu = lax.optimization_barrier(part_gu.astype(jnp.bfloat16)).astype(jnp.float32)
        part_dn = jnp.einsum("grh,grd->ghd", hidden_act.astype(jnp.float32).reshape(N_DP, group_rows, FF), scaled.astype(jnp.float32).reshape(N_DP, group_rows, D), precision=lax.Precision.HIGHEST)
        part_dn = lax.optimization_barrier(part_dn.astype(jnp.bfloat16)).astype(jnp.float32)
        return row_grad, prob_grad, jnp.sum(part_gu, axis=0), jnp.sum(part_dn, axis=0)

    row_grads, prob_grads, grad_gu, grad_dn = lax.map(one_expert, (table, weight_table, w_gate_up, w_down))
    grad_tokens = jnp.sum(row_grads[routes, place].astype(jnp.float32), axis=1)
    grad_weight = prob_grads[routes, place].astype(jnp.float32)
    expert_ids = jnp.arange(EXPERTS, dtype=jnp.int32)
    home = jnp.where(swap_flags == 1, jnp.bitwise_xor(expert_ids, EXPERTS // 2), expert_ids).astype(jnp.int32)
    return grad_tokens, grad_weight, grad_gu[home], grad_dn[home]
```

```python
import functools

import jax
import jax.numpy as jnp
from jax import lax
from jax.experimental import pallas as pl
from jax.experimental.pallas import tpu as pltpu
from jax.sharding import PartitionSpec as P

BF = jnp.bfloat16
F32 = jnp.float32
MESH = pl.DeviceIdType.MESH
GROUPS = 4
SLOTS = 8
LANES = 128
VMEM_BYTES = 60 * 2**20

ROWS_BY_ROWS = (((1,), (1,)), ((), ()))
COLS_BY_COLS = (((0,), (0,)), ((), ()))


def pick_tile(width, largest):
    tile = min(width, largest)
    while width % tile:
        tile -= LANES
    return tile


def exchange_kernel(
    sizes, hr_ref, idx_ref, weight_ref, flag_ref, tok_ref, cot_ref, wg_ref, wd_ref,
    ret_ref, own_g, own_d, far_g, far_d,
    sendb, recvb, mig_g, mig_d, full_g, full_d, rows_b, scaled_b, hid_b, both_b,
    retb, part_g, part_d, sib_g, sib_d,
    a2a_send, a2a_recv, ret_send, ret_recv,
    mig_send, mig_recv, far_send, far_recv, sib_send, sib_recv, fwd_send, fwd_recv,
    red_send, red_recv, out_send, out_recv,
):
    experts, width, ff = sizes
    block = experts // GROUPS
    chunk = block * SLOTS
    half = width // 2
    quarter_g, quarter_d = width // 4, ff // 4
    dp = lax.axis_index("dp")
    me = lax.axis_index("expert")
    my_group = me // block
    sib, far = dp ^ 1, dp ^ 2

    def remote(src, dst, send, recv, where):
        return pltpu.make_async_remote_copy(
            src_ref=src, dst_ref=dst, send_sem=send, recv_sem=recv,
            device_id=where, device_id_type=MESH,
        )

    step = quarter_g // 4
    pieces = [(True, k * step, step) for k in range(4)] + [(False, 0, quarter_d)]
    swaps = []
    for k, (is_g, off, count) in enumerate(pieces):
        src, dst = (wg_ref, mig_g) if is_g else (wd_ref, mig_d)
        copy = remote(
            src.at[pl.ds(off, count)], dst.at[pl.ds(off, count)],
            mig_send.at[k], mig_recv.at[k], (dp, me ^ (experts // 2)),
        )
        copy.start()
        swaps.append(copy)

    prep_tile = pick_tile(width, 512)

    def dispatch(g, carry):
        first = (my_group ^ g) * block
        codes = hr_ref[pl.ds(pl.multiple_of(first * SLOTS, SLOTS), chunk), :]
        pick = jnp.zeros((chunk, idx_ref.shape[1]), F32)
        pick_w = jnp.zeros((chunk, idx_ref.shape[1]), F32)
        for k in range(3):
            hit = codes == idx_ref[k : k + 1, :]
            pick = jnp.where(hit, 1.0, pick)
            pick_w = jnp.where(hit, weight_ref[k : k + 1, :], pick_w)
        pick = pick.astype(BF)
        pick_w = pick_w.astype(BF)
        for c in range(0, width, prep_tile):
            cols = slice(c, c + prep_tile)
            rows = jnp.dot(pick, tok_ref[:, cols], preferred_element_type=F32)
            cots = jnp.dot(pick_w, cot_ref[:, cols], preferred_element_type=F32)
            both = jnp.concatenate(
                [rows.reshape(block, SLOTS, prep_tile), cots.reshape(block, SLOTS, prep_tile)],
                axis=1,
            )
            sendb[pl.ds(first, block), :, cols] = both.astype(BF)

        def send(i, carry):
            peer = me ^ (g * block + i)

            @pl.when(peer != me)
            def _():
                remote(
                    sendb.at[peer], recvb.at[me], a2a_send, a2a_recv.at[g], (dp, peer)
                ).start()

            @pl.when(peer == me)
            def _():
                pltpu.make_async_copy(sendb.at[me], recvb.at[me], a2a_recv.at[g]).start()

            return carry

        return lax.fori_loop(0, block, send, carry)

    lax.fori_loop(0, GROUPS, dispatch, 0)

    lane = lax.broadcasted_iota(jnp.int32, flag_ref.shape, 1)
    mine = jnp.where(lane == me, flag_ref[...], 0)
    flagged = jnp.max(mine, axis=1, keepdims=True) == 1
    fars, sibs = [], []
    for k, (is_g, off, count) in enumerate(pieces):
        swaps[k].wait_recv()
        if is_g:
            own, mig, full, quarter = wg_ref, mig_g, full_g, quarter_g
        else:
            own, mig, full, quarter = wd_ref, mig_d, full_d, quarter_d
        chosen = jnp.where(flagged, mig[pl.ds(off, count), :], own[pl.ds(off, count), :])
        place = pl.ds(pl.multiple_of(dp * quarter + off, 16), count)
        full[place, :] = chosen
        copy = remote(full.at[place], full.at[place], far_send.at[k], far_recv.at[k], (far, me))
        copy.start()
        fars.append(copy)
        copy = remote(full.at[place], full.at[place], sib_send.at[k], sib_recv.at[k], (sib, me))
        copy.start()
        sibs.append(copy)
    fwds = []
    for k, (is_g, off, count) in enumerate(pieces):
        fars[k].wait_recv()
        full, quarter = (full_g, quarter_g) if is_g else (full_d, quarter_d)
        place = pl.ds(pl.multiple_of(far * quarter + off, 16), count)
        copy = remote(full.at[place], full.at[place], fwd_send.at[k], fwd_recv.at[k], (sib, me))
        copy.start()
        fwds.append(copy)
    for k in range(len(pieces)):
        sibs[k].wait_recv()
        fwds[k].wait_recv()

    ff_tile = pick_tile(ff, 256)
    half_tile = pick_tile(half, 256)

    def expert(g, carry):
        first = (my_group ^ g) * block
        arrived = recvb.at[pl.ds(first, block)]
        pltpu.make_async_copy(arrived, arrived, a2a_recv.at[g]).wait()
        place = pl.ds(pl.multiple_of(g * chunk, chunk), chunk)
        for c in range(0, width, prep_tile):
            cols = slice(c, c + prep_tile)
            both = recvb[pl.ds(first, block), :, cols].astype(F32)
            rows_b[place, cols] = both[:, :SLOTS].reshape(chunk, prep_tile).astype(BF)
            scaled_b[place, cols] = both[:, SLOTS:].reshape(chunk, prep_tile).astype(BF)
        prob = jnp.zeros((chunk, 1), F32)
        for f in range(0, ff, ff_tile):
            cols = slice(f, f + ff_tile)
            up_cols = slice(ff + f, ff + f + ff_tile)
            rows = rows_b[place, :]
            gate = jnp.dot(rows, full_g[:, cols], preferred_element_type=F32)
            up = jnp.dot(rows, full_g[:, up_cols], preferred_element_type=F32)
            hgrad = lax.dot_general(
                scaled_b[place, :], full_d[cols, :], ROWS_BY_ROWS, preferred_element_type=F32
            )
            sig = jax.nn.sigmoid(gate)
            silu = gate * sig
            hid = (silu * up).astype(BF)
            hid_b[place, cols] = hid
            both_b[place, cols] = (hgrad * up * sig * (1.0 + gate * (1.0 - sig))).astype(BF)
            both_b[place, up_cols] = (hgrad * silu).astype(BF)
            prob = prob + jnp.sum(hid.astype(F32) * hgrad, axis=1, keepdims=True)
        for c in range(0, half, half_tile):
            lo = lax.dot_general(
                both_b[place, :], full_g[c : c + half_tile, :], ROWS_BY_ROWS,
                preferred_element_type=F32,
            )
            hi = lax.dot_general(
                both_b[place, :], full_g[half + c : half + c + half_tile, :], ROWS_BY_ROWS,
                preferred_element_type=F32,
            )
            both = jnp.concatenate(
                [lo.reshape(block, SLOTS, half_tile), hi.reshape(block, SLOTS, half_tile)], axis=1
            )
            retb[pl.ds(first, block), :, c : c + half_tile] = both.astype(BF)
        prob = jnp.broadcast_to(prob, (chunk, LANES))
        rough = prob.astype(BF).astype(F32)
        both = jnp.concatenate(
            [rough.reshape(block, SLOTS, LANES), (prob - rough).reshape(block, SLOTS, LANES)],
            axis=1,
        )
        retb[pl.ds(first, block), :, half : half + LANES] = both.astype(BF)

        def send(i, carry):
            peer = me ^ (g * block + i)

            @pl.when(peer != me)
            def _():
                remote(retb.at[peer], ret_ref.at[me], ret_send, ret_recv, (dp, peer)).start()

            @pl.when(peer == me)
            def _():
                pltpu.make_async_copy(retb.at[me], ret_ref.at[me], ret_recv).start()

            return carry

        return lax.fori_loop(0, block, send, carry)

    lax.fori_loop(0, GROUPS, expert, 0)

    wide = pick_tile(2 * ff, 768)
    d_tile = pick_tile(quarter_g, 256)

    def gate_up_grads(quarter):
        def tile(i, carry):
            start = pl.multiple_of(quarter * quarter_g + i * d_tile, d_tile)
            left = rows_b[:, pl.ds(start, d_tile)]
            for c in range(0, 2 * ff, wide):
                part_g[pl.ds(start, d_tile), c : c + wide] = lax.dot_general(
                    left, both_b[:, c : c + wide], COLS_BY_COLS, preferred_element_type=F32
                ).astype(BF)
            return carry

        lax.fori_loop(0, quarter_g // d_tile, tile, 0)

    def down_grads():
        for f in range(0, ff, ff_tile):
            for c in range(0, width, prep_tile):
                part_d[f : f + ff_tile, c : c + prep_tile] = lax.dot_general(
                    hid_b[:, f : f + ff_tile], scaled_b[:, c : c + prep_tile], COLS_BY_COLS,
                    preferred_element_type=F32,
                ).astype(BF)

    def place_of(quarter, rows):
        return pl.ds(pl.multiple_of(quarter * rows, 16), rows)

    reds = []

    def to_sibling(slot, part, rows, landing, quarter):
        copy = remote(
            part.at[place_of(quarter, rows)], landing.at[slot % 2],
            red_send.at[slot], red_recv.at[slot], (sib, me),
        )
        copy.start()
        reds.append(copy)

    outs = []

    def to_far(slot, part, rows, landing, out):
        reds[slot].wait_recv()
        total = part[place_of(far, rows), :].astype(F32) + landing[0].astype(F32)
        landing[0] = total.astype(BF)
        copy = remote(landing.at[0], out, out_send.at[slot // 2], out_recv.at[slot // 2], (far, me))
        copy.start()
        outs.append(copy)

    gate_up_grads(far ^ 1)
    to_sibling(0, part_g, quarter_g, sib_g, far ^ 1)
    gate_up_grads(far)
    to_far(0, part_g, quarter_g, sib_g, far_g)
    gate_up_grads(dp ^ 1)
    to_sibling(1, part_g, quarter_g, sib_g, dp ^ 1)
    down_grads()
    to_sibling(2, part_d, quarter_d, sib_d, far ^ 1)
    to_far(2, part_d, quarter_d, sib_d, far_d)
    to_sibling(3, part_d, quarter_d, sib_d, dp ^ 1)
    gate_up_grads(dp)
    reds[1].wait_recv()
    own_g[...] = (
        part_g[place_of(dp, quarter_g), :].astype(F32) + sib_g[1].astype(F32)
    ).astype(BF)
    reds[3].wait_recv()
    own_d[...] = (
        part_d[place_of(dp, quarter_d), :].astype(F32) + sib_d[1].astype(F32)
    ).astype(BF)

    others = sendb.at[pl.ds(0, experts - 1)]
    pltpu.make_async_copy(others, others, a2a_send).wait()
    for copy in swaps + fars + sibs + fwds + reds:
        copy.wait_send()
    others = retb.at[pl.ds(0, experts - 1)]
    pltpu.make_async_copy(others, others, ret_send).wait()
    pltpu.make_async_copy(retb, retb, ret_recv).wait()
    for copy in outs:
        copy.wait()


def combine_kernel(ret_ref, idx_ref, weight_ref, hr_ref, tok_out, weight_out):
    experts, _, cols = ret_ref.shape
    half = cols - LANES
    rows = experts * SLOTS
    hits = [hr_ref[0:1, :] == idx_ref[:, k : k + 1] for k in range(3)]
    pick = jnp.zeros(hits[0].shape, F32)
    for hit in hits:
        pick = jnp.where(hit, 1.0, pick)
    pick = pick.astype(BF)
    tile = pick_tile(half, 512)
    for c in range(0, half, tile):
        both = ret_ref[:, :, c : c + tile].astype(F32)
        lo = both[:, :SLOTS].reshape(rows, tile).astype(BF)
        hi = both[:, SLOTS:].reshape(rows, tile).astype(BF)
        tok_out[:, c : c + tile] = jnp.dot(pick, lo, preferred_element_type=F32)
        tok_out[:, half + c : half + c + tile] = jnp.dot(pick, hi, preferred_element_type=F32)
    both = ret_ref[:, :, half:].astype(F32)
    rough = both[:, :SLOTS].reshape(rows, LANES).astype(BF)
    rest = both[:, SLOTS:].reshape(rows, LANES).astype(BF)
    for k in range(3):
        one = jnp.where(hits[k], 1.0, 0.0).astype(BF)
        prob = jnp.dot(one, rough, preferred_element_type=F32)
        prob = prob + jnp.dot(one, rest, preferred_element_type=F32)
        weight_out[:, k : k + 1] = prob[:, 0:1] / weight_ref[:, k : k + 1]


def body(tokens, cotangent, routes, slot_index, route_weight, swap_flags, w_gate_up, w_down):
    tok_rows, width = tokens.shape
    experts = swap_flags.shape[0]
    ff = w_down.shape[1] * lax.axis_size("dp")
    rows = experts * SLOTS
    quarter_g, quarter_d = w_gate_up.shape[1], w_down.shape[1]
    pieces = 5

    idx = routes * SLOTS + slot_index
    weight = route_weight.astype(BF).astype(F32)
    hr = jnp.arange(rows, dtype=jnp.int32) ^ (jnp.repeat(swap_flags, SLOTS) * (rows // 2))

    vmem = pl.BlockSpec(memory_space=pltpu.VMEM)
    hbm = pl.BlockSpec(memory_space=pl.ANY)
    dma = pltpu.SemaphoreType.DMA
    flops = 2 * rows * width * ff * 9
    ret, own_g, own_d, far_g, far_d = pl.pallas_call(
        functools.partial(exchange_kernel, (experts, width, ff)),
        name="exchange",
        out_shape=(
            jax.ShapeDtypeStruct((experts, 2 * SLOTS, width // 2 + LANES), BF),
            jax.ShapeDtypeStruct((quarter_g, 2 * ff), BF),
            jax.ShapeDtypeStruct((quarter_d, width), BF),
            jax.ShapeDtypeStruct((quarter_g, 2 * ff), BF),
            jax.ShapeDtypeStruct((quarter_d, width), BF),
        ),
        in_specs=[vmem] * 8,
        out_specs=(hbm, vmem, vmem, hbm, hbm),
        scratch_shapes=[
            pltpu.VMEM((experts, 2 * SLOTS, width), BF),
            pltpu.VMEM((experts, 2 * SLOTS, width), BF),
            pltpu.VMEM((quarter_g, 2 * ff), BF),
            pltpu.VMEM((quarter_d, width), BF),
            pltpu.VMEM((width, 2 * ff), BF),
            pltpu.VMEM((ff, width), BF),
            pltpu.VMEM((rows, width), BF),
            pltpu.VMEM((rows, width), BF),
            pltpu.VMEM((rows, ff), BF),
            pltpu.VMEM((rows, 2 * ff), BF),
            pltpu.VMEM((experts, 2 * SLOTS, width // 2 + LANES), BF),
            pltpu.VMEM((width, 2 * ff), BF),
            pltpu.VMEM((ff, width), BF),
            pltpu.VMEM((2, quarter_g, 2 * ff), BF),
            pltpu.VMEM((2, quarter_d, width), BF),
            dma, dma((GROUPS,)), dma, dma,
            dma((pieces,)), dma((pieces,)), dma((pieces,)), dma((pieces,)),
            dma((pieces,)), dma((pieces,)), dma((pieces,)), dma((pieces,)),
            dma((4,)), dma((4,)), dma((2,)), dma((2,)),
        ],
        compiler_params=pltpu.CompilerParams(
            has_side_effects=True, vmem_limit_bytes=VMEM_BYTES
        ),
        cost_estimate=pl.CostEstimate(
            flops=flops, bytes_accessed=12 * 2**20, transcendentals=rows * ff
        ),
    )(
        hr[:, None], idx.T, weight.T, swap_flags[None], tokens, cotangent, w_gate_up[0], w_down[0]
    )

    grad_tokens, grad_weight = pl.pallas_call(
        combine_kernel,
        name="combine",
        out_shape=(
            jax.ShapeDtypeStruct((tok_rows, width), F32),
            jax.ShapeDtypeStruct((tok_rows, 3), F32),
        ),
        in_specs=[vmem] * 4,
        out_specs=(vmem, vmem),
        compiler_params=pltpu.CompilerParams(vmem_limit_bytes=32 * 2**20),
    )(ret, idx, weight, hr[None])
    grad_gu = (own_g.astype(F32) + far_g.astype(F32))[None]
    grad_dn = (own_d.astype(F32) + far_d.astype(F32))[None]
    return (grad_tokens, grad_weight, grad_gu, grad_dn)


def solution(mesh):
    return jax.shard_map(
        body,
        mesh=mesh,
        in_specs=(
            P(("dp", "expert"), None),
            P(("dp", "expert"), None),
            P(("dp", "expert"), None),
            P(("dp", "expert"), None),
            P(("dp", "expert"), None),
            P(),
            P("expert", "dp", None),
            P("expert", "dp", None),
        ),
        out_specs=(
            P(("dp", "expert"), None),
            P(("dp", "expert"), None),
            P("expert", "dp", None),
            P("expert", "dp", None),
        ),
        check_vma=False,
    )
```

```python
import functools

import jax
import jax.numpy as jnp
from jax import lax
from jax.experimental import pallas as pl
from jax.experimental.pallas import tpu as pltpu
from jax.sharding import PartitionSpec as P

BF = jnp.bfloat16
F32 = jnp.float32
MESH = pl.DeviceIdType.MESH
GX, GZ, GY = 4, 8, 2
CHUNKS = 4
PIECES_G, PIECES_D = 8, 4
CFG = dict(ahead=6, first=12, per=6, lag=6)
SLOTS = 8
LANES = 128
VMEM_BYTES = 60 * 2**20

ROWS_BY_ROWS = (((1,), (1,)), ((), ()))
COLS_BY_COLS = (((0,), (0,)), ((), ()))


def pick_tile(width, largest):
    tile = min(width, largest)
    while width % tile:
        tile -= LANES
    return tile


def offsets_of(i):
    place, code = i // (GX * GY), i % (GX * GY)
    odd = place % 2
    dz = odd * ((place + 1) // 2) + (1 - odd) * ((GZ - place // 2) % GZ)
    return code // GY, dz, code % GY


def shifted(me, dx, dz, dy):
    x, z, y = me // (GZ * GY), (me // GY) % GZ, me % GY
    return ((x + dx) % GX) * (GZ * GY) + ((z + dz) % GZ) * GY + (y + dy) % GY


def partner(me, i, sign):
    dx, dz, dy = offsets_of(i)
    if sign < 0:
        dx, dz = GX - dx, GZ - dz
    return shifted(me, dx, dz, dy)


def replica(dp, i):
    crosses = (i % GY) * (dp % 2)
    return dp + crosses * (2 - 4 * (dp // 2))


def codes_of(me, first, rows, dim, flag_ref):
    experts = flag_ref.shape[1]
    if dim == 0:
        row = first + lax.broadcasted_iota(jnp.int32, (rows, experts), 0)
        slot = shifted(me, row // (SLOTS * GY), 0, (row // SLOTS) % GY)
        lane = lax.broadcasted_iota(jnp.int32, (rows, experts), 1)
        hit = jnp.where(lane == slot, 1.0, 0.0) * flag_ref[...].astype(F32)
        moved = jnp.max(hit, axis=1, keepdims=True)
        row, slot = row[:, :1], slot[:, :1]
    else:
        row = first + lax.broadcasted_iota(jnp.int32, (experts, rows), 1)
        slot = partner(me, row // SLOTS, 1)
        line = lax.broadcasted_iota(jnp.int32, (experts, rows), 0)
        hit = jnp.where(line == slot, 1.0, 0.0).astype(BF)
        flags = jnp.broadcast_to(flag_ref[...].astype(F32), (16, experts)).astype(BF)
        moved = jnp.dot(flags, hit, preferred_element_type=F32)[:1, :]
        row, slot = row[:1, :], slot[:1, :]
    home = jnp.where(moved > 0.5, slot ^ (experts // 2), slot)
    return home * SLOTS + row % SLOTS


def exchange_kernel(
    parts, sizes, route_ref, slot_ref, weight_ref, flag_ref, tok_ref, cot_ref, wg_ref, wd_ref,
    ret_ref, own_g, own_d, far_g, far_d,
    sendb, recvb, mig_g, mig_d, full_g, full_d, rows_b, scaled_b, hid_b, both_b,
    retb, part_g, sib_g, sib_d, gathered, meta,
    ring_send, ring_recv, meta_send, meta_recv, a2a_send, a2a_recv, ret_send, ret_recv,
    mig_send, mig_recv, far_send, far_recv, sib_send, sib_recv, fwd_send, fwd_recv,
    red_send, red_recv, out_send, out_recv,
):
    experts, width, ff = sizes
    block = experts // CHUNKS
    chunk = block * SLOTS
    half = width // 2
    quarter_g, quarter_d = width // 4, ff // 4
    tokens = tok_ref.shape[0]
    dp = lax.axis_index("dp")
    me = lax.axis_index("expert")
    sib, far = dp ^ 1, dp ^ 2

    def remote(src, dst, send, recv, where):
        return pltpu.make_async_remote_copy(
            src_ref=src, dst_ref=dst, send_sem=send, recv_sem=recv,
            device_id=where, device_id_type=MESH,
        )

    step_g, step_d = quarter_g // PIECES_G, quarter_d // PIECES_D
    pieces = [(True, k * step_g, step_g) for k in range(PIECES_G)]
    pieces += [(False, k * step_d, step_d) for k in range(PIECES_D)]
    if "W" not in parts:
        pieces = []
    swaps, fars, sibs, fwds = [], [], [], []

    def swap(k):
        if k >= len(pieces):
            return
        is_g, off, count = pieces[k]
        src, dst = (wg_ref, mig_g) if is_g else (wd_ref, mig_d)
        rows = pl.ds(off, count)
        copy = remote(
            src.at[rows], dst.at[rows], mig_send.at[k], mig_recv.at[k], (dp, me ^ (experts // 2))
        )
        copy.start()
        swaps.append(copy)

    def gather(k):
        is_g, off, count = pieces[k]
        if is_g:
            own, mig, full, quarter = wg_ref, mig_g, full_g, quarter_g
        else:
            own, mig, full, quarter = wd_ref, mig_d, full_d, quarter_d
        swaps[k].wait_recv()
        rows = pl.ds(off, count)
        place = pl.ds(pl.multiple_of(dp * quarter + off, 16), count)
        full[place, :] = jnp.where(flagged, mig[rows, :], own[rows, :])
        copy = remote(full.at[place], full.at[place], far_send.at[k], far_recv.at[k], (far, me))
        copy.start()
        fars.append(copy)
        copy = remote(full.at[place], full.at[place], sib_send.at[k], sib_recv.at[k], (sib, me))
        copy.start()
        sibs.append(copy)

    def forward(k):
        is_g, off, count = pieces[k]
        full, quarter = (full_g, quarter_g) if is_g else (full_d, quarter_d)
        fars[k].wait_recv()
        place = pl.ds(pl.multiple_of(far * quarter + off, 16), count)
        copy = remote(full.at[place], full.at[place], fwd_send.at[k], fwd_recv.at[k], (sib, me))
        copy.start()
        fwds.append(copy)

    prep_tile = pick_tile(width, 512)
    plane = GX * GY
    picked = plane * SLOTS

    def rows_at(dz, part):
        return pl.ds((2 * (dz - 1) + part) * tokens, tokens)

    def block_at(dz, part):
        return gathered.at[rows_at(dz, part)]

    def hop(src, dz, part, way):
        where = (dp, shifted(me, 0, way % GZ, 0))
        k = 2 * (dz - 1) + part
        copy = remote(src, block_at(dz, part), ring_send.at[k], ring_recv.at[k], where)
        copy.start()
        hops.append(copy)

    def landed(dz, part):
        k = 2 * (dz - 1) + part
        here = block_at(dz, part)
        pltpu.make_async_copy(here, here, ring_recv.at[k]).wait()
        if dz < GZ // 2 - 1 or (dz == GZ // 2 - 1 and part == 0):
            hop(here, dz + 1, part, 1)
        if dz > GZ // 2 + 1 or (dz == GZ // 2 + 1 and part == 1):
            hop(here, dz - 1, part, -1)

    def dispatch(place):
        dz = offsets_of(place * plane)[1]
        pick = jnp.zeros((picked, tokens), F32)
        pick_w = jnp.zeros((picked, tokens), F32)
        for k in range(3):
            hit = codes == meta[dz, k : k + 1, :]
            pick = jnp.where(hit, 1.0, pick)
            pick_w = jnp.where(hit, meta[dz, 4 + k : 5 + k, :], pick_w)
        pick = pick.astype(BF)
        pick_w = pick_w.astype(BF)
        first = place * plane
        for col in range(0, width, prep_tile):
            cols = slice(col, col + prep_tile)
            tok = tok_ref[:, cols] if dz == 0 else gathered[rows_at(dz, 0), cols]
            cot = cot_ref[:, cols] if dz == 0 else gathered[rows_at(dz, 1), cols]
            rows = jnp.dot(pick, tok, preferred_element_type=F32)
            cots = jnp.dot(pick_w, cot, preferred_element_type=F32)
            both = jnp.concatenate(
                [rows.reshape(plane, SLOTS, prep_tile), cots.reshape(plane, SLOTS, prep_tile)],
                axis=1,
            )
            sendb[first : first + plane, :, cols] = both.astype(BF)
        chunk_sem = a2a_recv.at[first // block]
        pltpu.make_async_copy(sendb.at[first], recvb.at[first], chunk_sem).start()

        def send(j, carry):
            where = (replica(dp, j), shifted(me, j // GY, 0, j % GY))
            i = first + j
            remote(sendb.at[i], recvb.at[i], a2a_send, chunk_sem, where).start()
            return carry

        lax.fori_loop(1, plane, send, 0)

    ahead, lag = CFG['ahead'], CFG['lag']
    for k in range(ahead):
        swap(k)
    hops = []
    if "D" in parts:
        meta[0] = jnp.zeros((SLOTS, tokens), F32)
        for k in range(3):
            code = route_ref[k : k + 1, :] * SLOTS + slot_ref[k : k + 1, :]
            meta[0, k : k + 1, :] = code.astype(F32)
            meta[0, 4 + k : 5 + k, :] = weight_ref[k : k + 1, :].astype(BF).astype(F32)
        for part, src in ((0, tok_ref), (1, cot_ref)):
            hop(src, 1, part, 1)
            hop(src, GZ - 1, part, -1)

        def send_meta(dz, carry):
            where = (dp, shifted(me, 0, dz, 0))
            remote(meta.at[0], meta.at[dz], meta_send, meta_recv, where).start()
            return carry

        lax.fori_loop(1, GZ, send_meta, 0)
        codes = codes_of(me, 0, picked, 0, flag_ref).astype(F32)
    lane = lax.broadcasted_iota(jnp.int32, flag_ref.shape, 1)
    mine = jnp.where(lane == me, flag_ref[...], 0).astype(F32)
    flagged = jnp.max(mine, axis=1, keepdims=True) > 0.5

    done = 0

    def weights(count):
        nonlocal done
        for k in range(done, min(done + count, len(pieces) + lag)):
            if k < len(pieces):
                gather(k)
                swap(k + ahead)
            if k >= lag:
                forward(k - lag)
            done = k + 1

    if "D" in parts:
        dispatch(0)
        others = meta.at[pl.ds(1, GZ - 1)]
        pltpu.make_async_copy(others, others, meta_recv).wait()
        for t in range(1, GZ // 2):
            for part in range(2):
                landed(t, part)
                landed(GZ - t, part)
            dispatch(2 * t - 1)
            dispatch(2 * t)
            weights(CFG["per"])
        for part in range(2):
            landed(GZ // 2, part)
        dispatch(GZ - 1)
    weights(len(pieces) + lag)
    for k in range(len(pieces)):
        sibs[k].wait_recv()
        fwds[k].wait_recv()

    ff_tile = pick_tile(ff, 256)
    half_tile = pick_tile(half, 256)

    def expert(c):
        first = c * block
        place = pl.ds(c * chunk, chunk)
        for col in range(0, width, prep_tile):
            cols = slice(col, col + prep_tile)
            both = recvb[pl.ds(first, block), :, cols].astype(F32)
            rows_b[place, cols] = both[:, :SLOTS].reshape(chunk, prep_tile).astype(BF)
            scaled_b[place, cols] = both[:, SLOTS:].reshape(chunk, prep_tile).astype(BF)
        prob = jnp.zeros((chunk, 1), F32)
        for f in range(0, ff, ff_tile):
            cols = slice(f, f + ff_tile)
            up_cols = slice(ff + f, ff + f + ff_tile)
            rows = rows_b[place, :]
            gate = jnp.dot(rows, full_g[:, cols], preferred_element_type=F32)
            up = jnp.dot(rows, full_g[:, up_cols], preferred_element_type=F32)
            hgrad = lax.dot_general(
                scaled_b[place, :], full_d[cols, :], ROWS_BY_ROWS, preferred_element_type=F32
            )
            sig = jax.nn.sigmoid(gate)
            silu = gate * sig
            hid = (silu * up).astype(BF)
            hid_b[place, cols] = hid
            both_b[place, cols] = (hgrad * up * sig * (1.0 + gate * (1.0 - sig))).astype(BF)
            both_b[place, up_cols] = (hgrad * silu).astype(BF)
            prob = prob + jnp.sum(hid.astype(F32) * hgrad, axis=1, keepdims=True)
        prob = jnp.broadcast_to(prob, (chunk, LANES))
        rough = prob.astype(BF).astype(F32)
        both = jnp.concatenate(
            [rough.reshape(block, SLOTS, LANES), (prob - rough).reshape(block, SLOTS, LANES)],
            axis=1,
        )
        retb[pl.ds(first, block), :, half : half + LANES] = both.astype(BF)

    def row_grads(c):
        first = c * block
        place = pl.ds(c * chunk, chunk)
        for col in range(0, half, half_tile):
            lo = lax.dot_general(
                both_b[place, :], full_g[col : col + half_tile, :], ROWS_BY_ROWS,
                preferred_element_type=F32,
            )
            hi = lax.dot_general(
                both_b[place, :], full_g[half + col : half + col + half_tile, :], ROWS_BY_ROWS,
                preferred_element_type=F32,
            )
            both = jnp.concatenate(
                [lo.reshape(block, SLOTS, half_tile), hi.reshape(block, SLOTS, half_tile)], axis=1
            )
            retb[pl.ds(first, block), :, col : col + half_tile] = both.astype(BF)

    def give_back(c):
        if "R" not in parts:
            return

        def send(j, carry):
            i = c * block + j

            @pl.when(i > 0)
            def _():
                remote(
                    retb.at[i], ret_ref.at[i], ret_send, ret_recv,
                    (replica(dp, i), partner(me, i, -1)),
                ).start()

            return carry

        lax.fori_loop(0, block, send, 0)

    def arrive(c):
        if "D" in parts:
            arrived = recvb.at[pl.ds(c * block, block)]
            pltpu.make_async_copy(arrived, arrived, a2a_recv.at[c]).wait()

    def early(c, carry):
        first = recvb.at[pl.ds(c * block, block)]
        if "D" in parts:
            pltpu.make_async_copy(first, first, a2a_recv.at[c]).wait()
        if "C" in parts:
            expert(c)
            row_grads(c)
        give_back(c)
        return carry

    lax.fori_loop(0, CHUNKS - 1, early, 0)
    if "R" in parts:
        pltpu.make_async_copy(retb.at[0], ret_ref.at[0], ret_recv).start()
    last = CHUNKS - 1
    arrive(last)
    if "C" in parts:
        expert(last)

    wide = pick_tile(2 * ff, 768)
    d_tile = pick_tile(quarter_g, 256)

    def gate_up_grads(quarter):
        if "G" not in parts:
            return

        def tile(i, carry):
            start = pl.multiple_of(quarter * quarter_g + i * d_tile, d_tile)
            left = rows_b[:, pl.ds(start, d_tile)]
            for c in range(0, 2 * ff, wide):
                part_g[pl.ds(start, d_tile), c : c + wide] = lax.dot_general(
                    left, both_b[:, c : c + wide], COLS_BY_COLS, preferred_element_type=F32
                ).astype(BF)
            return carry

        lax.fori_loop(0, quarter_g // d_tile, tile, 0)

    part_d = gathered

    def down_grads():
        for copy in hops:
            copy.wait_send()
        if "G" not in parts:
            return
        for f in range(0, ff, ff_tile):
            for c in range(0, width, prep_tile):
                part_d[f : f + ff_tile, c : c + prep_tile] = lax.dot_general(
                    hid_b[:, f : f + ff_tile], scaled_b[:, c : c + prep_tile], COLS_BY_COLS,
                    preferred_element_type=F32,
                ).astype(BF)

    def place_of(quarter, rows):
        return pl.ds(pl.multiple_of(quarter * rows, 16), rows)

    reds = []

    def to_sibling(slot, part, rows, landing, quarter, where):
        if "S" not in parts:
            return
        copy = remote(
            part.at[place_of(quarter, rows)], landing.at[where],
            red_send.at[slot], red_recv.at[slot], (sib, me),
        )
        copy.start()
        reds.append(copy)

    outs = []

    def to_far(slot, part, rows, landing, out):
        if "S" not in parts:
            return
        reds[slot].wait_recv()
        total = part[place_of(far, rows), :].astype(F32) + landing[0].astype(F32)
        landing[0] = total.astype(BF)
        copy = remote(landing.at[0], out, out_send.at[slot], out_recv.at[slot], (far, me))
        copy.start()
        outs.append(copy)

    gate_up_grads(far ^ 1)
    to_sibling(0, part_g, quarter_g, sib_g, far ^ 1, 0)
    gate_up_grads(far)
    to_far(0, part_g, quarter_g, sib_g, far_g)
    if "C" in parts:
        row_grads(last)
    give_back(last)
    down_grads()
    to_sibling(1, part_d, quarter_d, sib_d, far ^ 1, 0)
    to_sibling(2, part_d, quarter_d, sib_d, dp ^ 1, 1)
    gate_up_grads(dp ^ 1)
    to_sibling(3, part_g, quarter_g, sib_g, dp ^ 1, 1)
    to_far(1, part_d, quarter_d, sib_d, far_d)
    gate_up_grads(dp)
    if "S" in parts:
        reds[2].wait_recv()
        own_d[...] = (
            part_d[place_of(dp, quarter_d), :].astype(F32) + sib_d[1].astype(F32)
        ).astype(BF)
        reds[3].wait_recv()
        own_g[...] = (
            part_g[place_of(dp, quarter_g), :].astype(F32) + sib_g[1].astype(F32)
        ).astype(BF)

    if "D" in parts:
        others = sendb.at[pl.ds(0, experts - GZ)]
        pltpu.make_async_copy(others, others, a2a_send).wait()
        others = meta.at[pl.ds(1, GZ - 1)]
        pltpu.make_async_copy(others, others, meta_send).wait()
    for copy in swaps + fars + sibs + fwds + reds:
        copy.wait_send()
    if "R" in parts:
        others = retb.at[pl.ds(1, experts - 1)]
        pltpu.make_async_copy(others, others, ret_send).wait()
        pltpu.make_async_copy(retb, retb, ret_recv).wait()
    for copy in outs:
        copy.wait()


def combine_kernel(ret_ref, route_ref, slot_ref, weight_ref, flag_ref, tok_out, weight_out):
    experts, _, cols = ret_ref.shape
    half = cols - LANES
    rows = experts * SLOTS
    codes = codes_of(lax.axis_index("expert"), 0, rows, 1, flag_ref)
    tokens = route_ref.shape[1]
    hits = []
    for k in range(3):
        code = (route_ref[k : k + 1, :] * SLOTS + slot_ref[k : k + 1, :]).astype(F32)
        hits.append(codes == jnp.broadcast_to(code, (LANES, tokens)).T[:, :1].astype(jnp.int32))
    pick = jnp.zeros(hits[0].shape, F32)
    for hit in hits:
        pick = jnp.where(hit, 1.0, pick)
    pick = pick.astype(BF)
    tile = pick_tile(half, 512)
    for c in range(0, half, tile):
        both = ret_ref[:, :, c : c + tile].astype(F32)
        lo = both[:, :SLOTS].reshape(rows, tile).astype(BF)
        hi = both[:, SLOTS:].reshape(rows, tile).astype(BF)
        tok_out[:, c : c + tile] = jnp.dot(pick, lo, preferred_element_type=F32)
        tok_out[:, half + c : half + c + tile] = jnp.dot(pick, hi, preferred_element_type=F32)
    both = ret_ref[:, :, half:].astype(F32)
    rough = both[:, :SLOTS].reshape(rows, LANES).astype(BF)
    rest = both[:, SLOTS:].reshape(rows, LANES).astype(BF)
    for k in range(3):
        one = jnp.where(hits[k], 1.0, 0.0).astype(BF)
        prob = jnp.dot(one, rough, preferred_element_type=F32)
        prob = prob + jnp.dot(one, rest, preferred_element_type=F32)
        weight_out[k : k + 1, :] = prob.T[:1, :] / weight_ref[k : k + 1, :].astype(BF).astype(F32)


def body(parts, tokens, cotangent, routes, slot_index, route_weight, swap_flags, w_gate_up, w_down):
    tok_rows, width = tokens.shape
    experts = swap_flags.shape[0]
    ff = w_down.shape[1] * lax.axis_size("dp")
    rows = experts * SLOTS
    quarter_g, quarter_d = w_gate_up.shape[1], w_down.shape[1]
    pieces = PIECES_G + PIECES_D

    vmem = pl.BlockSpec(memory_space=pltpu.VMEM)
    hbm = pl.BlockSpec(memory_space=pl.ANY)
    dma = pltpu.SemaphoreType.DMA
    flops = 2 * rows * width * ff * 9
    ret, own_g, own_d, far_g, far_d = pl.pallas_call(
        functools.partial(exchange_kernel, parts, (experts, width, ff)),
        name="ex_" + "".join(parts),
        out_shape=(
            jax.ShapeDtypeStruct((experts, 2 * SLOTS, width // 2 + LANES), BF),
            jax.ShapeDtypeStruct((quarter_g, 2 * ff), BF),
            jax.ShapeDtypeStruct((quarter_d, width), BF),
            jax.ShapeDtypeStruct((quarter_g, 2 * ff), BF),
            jax.ShapeDtypeStruct((quarter_d, width), BF),
        ),
        in_specs=[vmem] * 8,
        out_specs=(hbm, vmem, vmem, hbm, hbm),
        scratch_shapes=[
            pltpu.VMEM((experts, 2 * SLOTS, width), BF),
            pltpu.VMEM((experts, 2 * SLOTS, width), BF),
            pltpu.VMEM((quarter_g, 2 * ff), BF),
            pltpu.VMEM((quarter_d, width), BF),
            pltpu.VMEM((width, 2 * ff), BF),
            pltpu.VMEM((ff, width), BF),
            pltpu.VMEM((rows, width), BF),
            pltpu.VMEM((rows, width), BF),
            pltpu.VMEM((rows, ff), BF),
            pltpu.VMEM((rows, 2 * ff), BF),
            pltpu.VMEM((experts, 2 * SLOTS, width // 2 + LANES), BF),
            pltpu.VMEM((width, 2 * ff), BF),
            pltpu.VMEM((2, quarter_g, 2 * ff), BF),
            pltpu.VMEM((2, quarter_d, width), BF),
            pltpu.VMEM((2 * (GZ - 1) * tok_rows, width), BF),
            pltpu.VMEM((GZ, SLOTS, tok_rows), F32),
            dma((2 * GZ - 2,)), dma((2 * GZ - 2,)), dma, dma,
            dma, dma((CHUNKS,)), dma, dma,
            dma((pieces,)), dma((pieces,)), dma((pieces,)), dma((pieces,)),
            dma((pieces,)), dma((pieces,)), dma((pieces,)), dma((pieces,)),
            dma((4,)), dma((4,)), dma((2,)), dma((2,)),
        ],
        compiler_params=pltpu.CompilerParams(
            has_side_effects=True, vmem_limit_bytes=VMEM_BYTES
        ),
        cost_estimate=pl.CostEstimate(
            flops=flops, bytes_accessed=12 * 2**20, transcendentals=rows * ff
        ),
    )(
        routes.T, slot_index.T, route_weight.T, swap_flags[None], tokens, cotangent, w_gate_up[0], w_down[0]
    )

    grad_tokens, grad_weight = pl.pallas_call(
        combine_kernel,
        name="combine",
        out_shape=(
            jax.ShapeDtypeStruct((tok_rows, width), F32),
            jax.ShapeDtypeStruct((3, tok_rows), F32),
        ),
        in_specs=[vmem] * 5,
        out_specs=(vmem, vmem),
        compiler_params=pltpu.CompilerParams(vmem_limit_bytes=32 * 2**20),
    )(ret, routes.T, slot_index.T, route_weight.T, swap_flags[None])
    grad_gu = (own_g.astype(F32) + far_g.astype(F32))[None]
    grad_dn = (own_d.astype(F32) + far_d.astype(F32))[None]
    return (grad_tokens, grad_weight.T, grad_gu, grad_dn)


def solution(mesh):
    return jax.shard_map(
        functools.partial(body, 'DWCGRS'),
        mesh=mesh,
        in_specs=(
            P(("dp", "expert"), None),
            P(("dp", "expert"), None),
            P(("dp", "expert"), None),
            P(("dp", "expert"), None),
            P(("dp", "expert"), None),
            P(),
            P("expert", "dp", None),
            P("expert", "dp", None),
        ),
        out_specs=(
            P(("dp", "expert"), None),
            P(("dp", "expert"), None),
            P("expert", "dp", None),
            P("expert", "dp", None),
        ),
        check_vma=False,
    )
```

```python
import functools

import jax
import jax.numpy as jnp
from jax import lax
from jax.experimental import pallas as pl
from jax.experimental.pallas import tpu as pltpu
from jax.sharding import PartitionSpec as P

BF = jnp.bfloat16
F32 = jnp.float32
MESH = pl.DeviceIdType.MESH
GX, GZ, GY = 4, 8, 2
CHUNKS = 4
PIECES_G, PIECES_D = 8, 4
AHEAD, FIRST = 12, 6
DEFER = 0
SLOTS = 8
LANES = 128
VMEM_BYTES = 61 * 2**20

ROWS_BY_ROWS = (((1,), (1,)), ((), ()))
COLS_BY_COLS = (((0,), (0,)), ((), ()))


def pick_tile(width, largest):
    tile = min(width, largest)
    while width % tile:
        tile -= LANES
    return tile


def offsets_of(i):
    place, code = i // (GX * GY), i % (GX * GY)
    odd = place % 2
    dz = odd * ((place + 1) // 2) + (1 - odd) * ((GZ - place // 2) % GZ)
    return code // GY, dz, code % GY


def shifted(me, dx, dz, dy):
    x, z, y = me // (GZ * GY), (me // GY) % GZ, me % GY
    return ((x + dx) % GX) * (GZ * GY) + ((z + dz) % GZ) * GY + (y + dy) % GY


def partner(me, i, sign):
    dx, dz, dy = offsets_of(i)
    if sign < 0:
        dx, dz = GX - dx, GZ - dz
    return shifted(me, dx, dz, dy)


def replica(dp, i):
    crosses = (i % GY) * (dp % 2)
    return dp + crosses * (2 - 4 * (dp // 2))


def codes_of(me, first, rows, dim, flag_ref):
    experts = flag_ref.shape[1]
    if dim == 0:
        row = first + lax.broadcasted_iota(jnp.int32, (rows, experts), 0)
        slot = shifted(me, row // (SLOTS * GY), 0, (row // SLOTS) % GY)
        lane = lax.broadcasted_iota(jnp.int32, (rows, experts), 1)
        hit = jnp.where(lane == slot, 1.0, 0.0) * flag_ref[...].astype(F32)
        moved = jnp.max(hit, axis=1, keepdims=True)
        row, slot = row[:, :1], slot[:, :1]
    else:
        row = first + lax.broadcasted_iota(jnp.int32, (experts, rows), 1)
        slot = partner(me, row // SLOTS, 1)
        line = lax.broadcasted_iota(jnp.int32, (experts, rows), 0)
        hit = jnp.where(line == slot, 1.0, 0.0).astype(BF)
        flags = jnp.broadcast_to(flag_ref[...].astype(F32), (16, experts)).astype(BF)
        moved = jnp.dot(flags, hit, preferred_element_type=F32)[:1, :]
        row, slot = row[:1, :], slot[:1, :]
    home = jnp.where(moved > 0.5, slot ^ (experts // 2), slot)
    return home * SLOTS + row % SLOTS


def exchange_kernel(
    parts, sizes, route_ref, slot_ref, weight_ref, flag_ref, tok_ref, cot_ref, wg_ref, wd_ref,
    ret_ref, own_g, own_d, far_g, far_d,
    sendb, recvb, mig_g, mig_d, full_g, full_d, rows_b, scaled_b, hid_b, both_b,
    retb, part_g, sib_g, sib_d, gathered, meta, gate_up,
    ring_send, ring_recv, meta_send, meta_recv, a2a_send, a2a_recv, ret_send, ret_recv,
    mig_send, mig_recv, far_send, far_recv, sib_send, sib_recv, fwd_send, fwd_recv,
    red_send, red_recv, out_send, out_recv,
):
    experts, width, ff = sizes
    block = experts // CHUNKS
    chunk = block * SLOTS
    half = width // 2
    quarter_g, quarter_d = width // 4, ff // 4
    tokens = tok_ref.shape[0]
    dp = lax.axis_index("dp")
    me = lax.axis_index("expert")
    sib, far = dp ^ 1, dp ^ 2

    def remote(src, dst, send, recv, where):
        return pltpu.make_async_remote_copy(
            src_ref=src, dst_ref=dst, send_sem=send, recv_sem=recv,
            device_id=where, device_id_type=MESH,
        )

    step_g, step_d = quarter_g // PIECES_G, quarter_d // PIECES_D
    pieces = [(True, k * step_g, step_g) for k in range(PIECES_G)]
    pieces += [(False, k * step_d, step_d) for k in range(PIECES_D)]
    if "W" not in parts:
        pieces = []
    swaps, fars, sibs, fwds = [], [], [], []

    def swap(k):
        if k >= len(pieces):
            return
        is_g, off, count = pieces[k]
        src, dst = (wg_ref, mig_g) if is_g else (wd_ref, mig_d)
        rows = pl.ds(off, count)
        copy = remote(
            src.at[rows], dst.at[rows], mig_send.at[k], mig_recv.at[k], (dp, me ^ (experts // 2))
        )
        copy.start()
        swaps.append(copy)

    def gather(k):
        is_g, off, count = pieces[k]
        if is_g:
            own, mig, full, quarter = wg_ref, mig_g, full_g, quarter_g
        else:
            own, mig, full, quarter = wd_ref, mig_d, full_d, quarter_d
        swaps[k].wait_recv()
        rows = pl.ds(off, count)
        place = pl.ds(pl.multiple_of(dp * quarter + off, 16), count)
        full[place, :] = jnp.where(flagged, mig[rows, :], own[rows, :])
        copy = remote(full.at[place], full.at[place], far_send.at[k], far_recv.at[k], (far, me))
        copy.start()
        fars.append(copy)
        copy = remote(full.at[place], full.at[place], sib_send.at[k], sib_recv.at[k], (sib, me))
        copy.start()
        sibs.append(copy)

    def forward(k):
        is_g, off, count = pieces[k]
        full, quarter = (full_g, quarter_g) if is_g else (full_d, quarter_d)
        fars[k].wait_recv()
        place = pl.ds(pl.multiple_of(far * quarter + off, 16), count)
        copy = remote(full.at[place], full.at[place], fwd_send.at[k], fwd_recv.at[k], (sib, me))
        copy.start()
        fwds.append(copy)

    prep_tile = pick_tile(width, 512)
    plane = GX * GY
    picked = plane * SLOTS

    def rows_at(dz, part):
        return pl.ds((2 * (dz - 1) + part) * tokens, tokens)

    def block_at(dz, part):
        return gathered.at[rows_at(dz, part)]

    def hop(src, dz, part, way):
        where = (dp, shifted(me, 0, way % GZ, 0))
        k = 2 * (dz - 1) + part
        copy = remote(src, block_at(dz, part), ring_send.at[k], ring_recv.at[k], where)
        copy.start()
        hops.append(copy)

    def landed(dz, part):
        k = 2 * (dz - 1) + part
        here = block_at(dz, part)
        pltpu.make_async_copy(here, here, ring_recv.at[k]).wait()
        if dz < GZ // 2 - 1 or (dz == GZ // 2 - 1 and part == 0):
            hop(here, dz + 1, part, 1)
        if dz > GZ // 2 + 1 or (dz == GZ // 2 + 1 and part == 1):
            hop(here, dz - 1, part, -1)

    def prepare(place):
        dz = offsets_of(place * plane)[1]
        pick = jnp.zeros((picked, tokens), F32)
        pick_w = jnp.zeros((picked, tokens), F32)
        for k in range(3):
            hit = codes == meta[dz, k : k + 1, :]
            pick = jnp.where(hit, 1.0, pick)
            pick_w = jnp.where(hit, meta[dz, 4 + k : 5 + k, :], pick_w)
        pick = pick.astype(BF)
        pick_w = pick_w.astype(BF)
        first = place * plane
        for col in range(0, width, prep_tile):
            cols = slice(col, col + prep_tile)
            tok = tok_ref[:, cols] if dz == 0 else gathered[rows_at(dz, 0), cols]
            cot = cot_ref[:, cols] if dz == 0 else gathered[rows_at(dz, 1), cols]
            rows = jnp.dot(pick, tok, preferred_element_type=F32)
            cots = jnp.dot(pick_w, cot, preferred_element_type=F32)
            both = jnp.concatenate(
                [rows.reshape(plane, SLOTS, prep_tile), cots.reshape(plane, SLOTS, prep_tile)],
                axis=1,
            )
            sendb[first : first + plane, :, cols] = both.astype(BF)

    def push(place):
        first = place * plane
        chunk_sem = a2a_recv.at[first // block]
        pltpu.make_async_copy(sendb.at[first], recvb.at[first], chunk_sem).start()

        def send(j, carry):
            where = (replica(dp, j), shifted(me, j // GY, 0, j % GY))
            i = first + j
            remote(sendb.at[i], recvb.at[i], a2a_send, chunk_sem, where).start()
            return carry

        lax.fori_loop(1, plane, send, 0)

    for k in range(AHEAD):
        swap(k)
    hops = []
    if "D" in parts:
        meta[0] = jnp.zeros((SLOTS, tokens), F32)
        for k in range(3):
            code = route_ref[k : k + 1, :] * SLOTS + slot_ref[k : k + 1, :]
            meta[0, k : k + 1, :] = code.astype(F32)
            meta[0, 4 + k : 5 + k, :] = weight_ref[k : k + 1, :].astype(BF).astype(F32)
        for part, src in ((0, tok_ref), (1, cot_ref)):
            hop(src, 1, part, 1)
            hop(src, GZ - 1, part, -1)

        def send_meta(dz, carry):
            where = (dp, shifted(me, 0, dz, 0))
            remote(meta.at[0], meta.at[dz], meta_send, meta_recv, where).start()
            return carry

        lax.fori_loop(1, GZ, send_meta, 0)
        codes = codes_of(me, 0, picked, 0, flag_ref).astype(F32)
    lane = lax.broadcasted_iota(jnp.int32, flag_ref.shape, 1)
    mine = jnp.where(lane == me, flag_ref[...], 0).astype(F32)
    flagged = jnp.max(mine, axis=1, keepdims=True) > 0.5

    ff_tile = pick_tile(ff, 256)
    half_tile = pick_tile(half, 256)

    def forward_part(first, count):
        rows_n = count * SLOTS
        place = pl.ds(first * SLOTS, rows_n)
        for col in range(0, width, prep_tile):
            cols = slice(col, col + prep_tile)
            both = recvb[first : first + count, :, cols].astype(F32)
            rows_b[place, cols] = both[:, :SLOTS].reshape(rows_n, prep_tile).astype(BF)
            scaled_b[place, cols] = both[:, SLOTS:].reshape(rows_n, prep_tile).astype(BF)
        for f in range(0, 2 * ff, ff_tile):
            cols = slice(f, f + ff_tile)
            gate_up[:rows_n, cols] = jnp.dot(
                rows_b[place, :], full_g[:, cols], preferred_element_type=F32
            )

    def backward_part(first, count):
        rows_n = count * SLOTS
        place = pl.ds(first * SLOTS, rows_n)
        prob = jnp.zeros((rows_n, 1), F32)
        for f in range(0, ff, ff_tile):
            cols = slice(f, f + ff_tile)
            up_cols = slice(ff + f, ff + f + ff_tile)
            gate, up = gate_up[:rows_n, cols], gate_up[:rows_n, up_cols]
            hgrad = lax.dot_general(
                scaled_b[place, :], full_d[cols, :], ROWS_BY_ROWS, preferred_element_type=F32
            )
            sig = jax.nn.sigmoid(gate)
            silu = gate * sig
            hid = (silu * up).astype(BF)
            hid_b[place, cols] = hid
            both_b[place, cols] = (hgrad * up * sig * (1.0 + gate * (1.0 - sig))).astype(BF)
            both_b[place, up_cols] = (hgrad * silu).astype(BF)
            prob = prob + jnp.sum(hid.astype(F32) * hgrad, axis=1, keepdims=True)
        prob = jnp.broadcast_to(prob, (rows_n, LANES))
        rough = prob.astype(BF).astype(F32)
        both = jnp.concatenate(
            [rough.reshape(count, SLOTS, LANES), (prob - rough).reshape(count, SLOTS, LANES)],
            axis=1,
        )
        retb[first : first + count, :, half : half + LANES] = both.astype(BF)

    def row_grads(first, count):
        place = pl.ds(first * SLOTS, count * SLOTS)
        for col in range(0, half, half_tile):
            lo = lax.dot_general(
                both_b[place, :], full_g[col : col + half_tile, :], ROWS_BY_ROWS,
                preferred_element_type=F32,
            )
            hi = lax.dot_general(
                both_b[place, :], full_g[half + col : half + col + half_tile, :], ROWS_BY_ROWS,
                preferred_element_type=F32,
            )
            both = jnp.concatenate(
                [lo.reshape(count, SLOTS, half_tile), hi.reshape(count, SLOTS, half_tile)], axis=1
            )
            retb[first : first + count, :, col : col + half_tile] = both.astype(BF)

    def give_back(c):
        if "R" not in parts:
            return

        def send(j, carry):
            i = c * block + j

            @pl.when(i > 0)
            def _():
                remote(
                    retb.at[i], ret_ref.at[i], ret_send, ret_recv,
                    (replica(dp, i), partner(me, i, -1)),
                ).start()

            return carry

        lax.fori_loop(0, block, send, 0)

    def arrive(c):
        if "D" in parts:
            arrived = recvb.at[pl.ds(c * block, block)]
            pltpu.make_async_copy(arrived, arrived, a2a_recv.at[c]).wait()

    def weights(gathers, forwards):
        for k in gathers:
            if k < len(pieces):
                gather(k)
                swap(k + AHEAD)
        for k in forwards:
            if k < len(pieces):
                forward(k)

    total = PIECES_G + PIECES_D
    plan = {
        1: (range(FIRST), ()),
        2: (range(FIRST, total), range(FIRST)),
        3: ((), range(FIRST, total)),
    }
    if "D" in parts:
        prepare(0)
        if DEFER == 0:
            push(0)
        others = meta.at[pl.ds(1, GZ - 1)]
        pltpu.make_async_copy(others, others, meta_recv).wait()
    for t in range(1, GZ // 2):
        if "D" in parts:
            for part in range(2):
                landed(t, part)
                landed(GZ - t, part)
        if t <= DEFER:
            weights(*plan[t])
        if "D" in parts:
            for place in (2 * t - 1, 2 * t):
                prepare(place)
                if t > DEFER:
                    push(place)
            if t == DEFER:
                for place in range(2 * t + 1):
                    push(place)
        if t > DEFER:
            weights(*plan[t])
    if "D" in parts:
        for part in range(2):
            landed(GZ // 2, part)
        prepare(GZ - 1)
        push(GZ - 1)

    def complete(first, stop):
        for k in range(first, min(stop, len(pieces))):
            sibs[k].wait_recv()
            fwds[k].wait_recv()

    last = CHUNKS - 1
    ahead = last * block
    for c in range(last):
        arrive(c)
    complete(0, PIECES_G)
    if "C" in parts:
        forward_part(0, ahead)
    complete(PIECES_G, total)
    if "C" in parts:
        backward_part(0, ahead)
        row_grads(0, ahead)
    if "R" in parts:
        pltpu.make_async_copy(retb.at[0], ret_ref.at[0], ret_recv).start()
    for c in range(last):
        give_back(c)
    arrive(last)
    if "C" in parts:
        forward_part(ahead, block)
        backward_part(ahead, block)

    wide = pick_tile(2 * ff, 768)
    d_tile = pick_tile(quarter_g, 256)

    def gate_up_grads(quarter):
        if "G" not in parts:
            return

        def tile(i, carry):
            start = pl.multiple_of(quarter * quarter_g + i * d_tile, d_tile)
            left = rows_b[:, pl.ds(start, d_tile)]
            for c in range(0, 2 * ff, wide):
                part_g[pl.ds(start, d_tile), c : c + wide] = lax.dot_general(
                    left, both_b[:, c : c + wide], COLS_BY_COLS, preferred_element_type=F32
                ).astype(BF)
            return carry

        lax.fori_loop(0, quarter_g // d_tile, tile, 0)

    part_d = gathered

    def down_grads():
        for copy in hops:
            copy.wait_send()
        if "G" not in parts:
            return
        for f in range(0, ff, ff_tile):
            for c in range(0, width, prep_tile):
                part_d[f : f + ff_tile, c : c + prep_tile] = lax.dot_general(
                    hid_b[:, f : f + ff_tile], scaled_b[:, c : c + prep_tile], COLS_BY_COLS,
                    preferred_element_type=F32,
                ).astype(BF)

    def place_of(quarter, rows):
        return pl.ds(pl.multiple_of(quarter * rows, 16), rows)

    reds = []

    def to_sibling(slot, part, rows, landing, quarter, where):
        if "S" not in parts:
            return
        copy = remote(
            part.at[place_of(quarter, rows)], landing.at[where],
            red_send.at[slot], red_recv.at[slot], (sib, me),
        )
        copy.start()
        reds.append(copy)

    outs = []

    def to_far(slot, part, rows, landing, out):
        if "S" not in parts:
            return
        reds[slot].wait_recv()
        total = part[place_of(far, rows), :].astype(F32) + landing[0].astype(F32)
        landing[0] = total.astype(BF)
        copy = remote(landing.at[0], out, out_send.at[slot], out_recv.at[slot], (far, me))
        copy.start()
        outs.append(copy)

    gate_up_grads(far ^ 1)
    to_sibling(0, part_g, quarter_g, sib_g, far ^ 1, 0)
    gate_up_grads(far)
    to_far(0, part_g, quarter_g, sib_g, far_g)
    if "C" in parts:
        row_grads(ahead, block)
    give_back(last)
    down_grads()
    to_sibling(1, part_d, quarter_d, sib_d, far ^ 1, 0)
    to_sibling(2, part_d, quarter_d, sib_d, dp ^ 1, 1)
    gate_up_grads(dp ^ 1)
    to_sibling(3, part_g, quarter_g, sib_g, dp ^ 1, 1)
    to_far(1, part_d, quarter_d, sib_d, far_d)
    gate_up_grads(dp)
    if "S" in parts:
        reds[2].wait_recv()
        own_d[...] = (
            part_d[place_of(dp, quarter_d), :].astype(F32) + sib_d[1].astype(F32)
        ).astype(BF)
        reds[3].wait_recv()
        own_g[...] = (
            part_g[place_of(dp, quarter_g), :].astype(F32) + sib_g[1].astype(F32)
        ).astype(BF)

    if "D" in parts:
        others = sendb.at[pl.ds(0, experts - GZ)]
        pltpu.make_async_copy(others, others, a2a_send).wait()
        others = meta.at[pl.ds(1, GZ - 1)]
        pltpu.make_async_copy(others, others, meta_send).wait()
    for copy in swaps + fars + sibs + fwds + reds:
        copy.wait_send()
    if "R" in parts:
        others = retb.at[pl.ds(1, experts - 1)]
        pltpu.make_async_copy(others, others, ret_send).wait()
        pltpu.make_async_copy(retb, retb, ret_recv).wait()
    for copy in outs:
        copy.wait()


def finish_kernel(
    ret_hbm, own_g, own_d, far_g, far_d, route_ref, slot_ref, weight_ref, flag_ref,
    tok_out, weight_out, out_g, out_d,
    ret_ref, a_g, b_g, a_d, b_d, sum_g, sum_d, tok_ref, in_sem, out_sem,
):
    experts, _, cols = ret_ref.shape
    half = cols - LANES
    rows = experts * SLOTS
    load_ret = pltpu.make_async_copy(ret_hbm, ret_ref, in_sem.at[0])
    load_ret.start()
    steps = 4
    step_g, step_d = a_g.shape[0] // steps, a_d.shape[0] // steps
    loads = []
    for k in range(steps):
        for n, (src, dst, step) in enumerate(
            ((own_g, a_g, step_g), (far_g, b_g, step_g), (own_d, a_d, step_d), (far_d, b_d, step_d))
        ):
            part = pl.ds(k * step, step)
            copy = pltpu.make_async_copy(src.at[part], dst.at[part], in_sem.at[1 + 4 * k + n])
            copy.start()
            loads.append(copy)
    codes = codes_of(lax.axis_index("expert"), 0, rows, 1, flag_ref)
    tokens = route_ref.shape[1]
    hits = []
    for k in range(3):
        code = (route_ref[k : k + 1, :] * SLOTS + slot_ref[k : k + 1, :]).astype(F32)
        hits.append(codes == jnp.broadcast_to(code, (LANES, tokens)).T[:, :1].astype(jnp.int32))
    pick = jnp.zeros(hits[0].shape, F32)
    for hit in hits:
        pick = jnp.where(hit, 1.0, pick)
    pick = pick.astype(BF)
    load_ret.wait()
    stores = []

    def store(src, dst, n):
        copy = pltpu.make_async_copy(src, dst, out_sem.at[n])
        copy.start()
        stores.append(copy)

    tile = pick_tile(half, 512)
    for c in range(0, half, tile):
        both = ret_ref[:, :, c : c + tile].astype(F32)
        lo = both[:, :SLOTS].reshape(rows, tile).astype(BF)
        hi = both[:, SLOTS:].reshape(rows, tile).astype(BF)
        tok_ref[:, c : c + tile] = jnp.dot(pick, lo, preferred_element_type=F32)
        tok_ref[:, half + c : half + c + tile] = jnp.dot(pick, hi, preferred_element_type=F32)
    store(tok_ref, tok_out, 0)
    for k in range(steps):
        for copy in loads[4 * k : 4 * k + 4]:
            copy.wait()
        part = pl.ds(k * step_g, step_g)
        sum_g[part, :] = a_g[part, :].astype(F32) + b_g[part, :].astype(F32)
        store(sum_g.at[part], out_g.at[part], 1 + 2 * k)
        part = pl.ds(k * step_d, step_d)
        sum_d[part, :] = a_d[part, :].astype(F32) + b_d[part, :].astype(F32)
        store(sum_d.at[part], out_d.at[part], 2 + 2 * k)
    both = ret_ref[:, :, half:].astype(F32)
    rough = both[:, :SLOTS].reshape(rows, LANES).astype(BF)
    rest = both[:, SLOTS:].reshape(rows, LANES).astype(BF)
    for k in range(3):
        one = jnp.where(hits[k], 1.0, 0.0).astype(BF)
        prob = jnp.dot(one, rough, preferred_element_type=F32)
        prob = prob + jnp.dot(one, rest, preferred_element_type=F32)
        weight_out[k : k + 1, :] = prob.T[:1, :] / weight_ref[k : k + 1, :].astype(BF).astype(F32)
    for copy in stores:
        copy.wait()


def body(parts, tokens, cotangent, routes, slot_index, route_weight, swap_flags, w_gate_up, w_down):
    tok_rows, width = tokens.shape
    experts = swap_flags.shape[0]
    ff = w_down.shape[1] * lax.axis_size("dp")
    rows = experts * SLOTS
    quarter_g, quarter_d = w_gate_up.shape[1], w_down.shape[1]
    pieces = PIECES_G + PIECES_D

    vmem = pl.BlockSpec(memory_space=pltpu.VMEM)
    hbm = pl.BlockSpec(memory_space=pl.ANY)
    dma = pltpu.SemaphoreType.DMA
    flops = 2 * rows * width * ff * 9
    ret, own_g, own_d, far_g, far_d = pl.pallas_call(
        functools.partial(exchange_kernel, parts, (experts, width, ff)),
        name="ex_" + "".join(parts),
        out_shape=(
            jax.ShapeDtypeStruct((experts, 2 * SLOTS, width // 2 + LANES), BF),
            jax.ShapeDtypeStruct((quarter_g, 2 * ff), BF),
            jax.ShapeDtypeStruct((quarter_d, width), BF),
            jax.ShapeDtypeStruct((quarter_g, 2 * ff), BF),
            jax.ShapeDtypeStruct((quarter_d, width), BF),
        ),
        in_specs=[vmem] * 8,
        out_specs=(hbm, vmem, vmem, hbm, hbm),
        scratch_shapes=[
            pltpu.VMEM((experts, 2 * SLOTS, width), BF),
            pltpu.VMEM((experts, 2 * SLOTS, width), BF),
            pltpu.VMEM((quarter_g, 2 * ff), BF),
            pltpu.VMEM((quarter_d, width), BF),
            pltpu.VMEM((width, 2 * ff), BF),
            pltpu.VMEM((ff, width), BF),
            pltpu.VMEM((rows, width), BF),
            pltpu.VMEM((rows, width), BF),
            pltpu.VMEM((rows, ff), BF),
            pltpu.VMEM((rows, 2 * ff), BF),
            pltpu.VMEM((experts, 2 * SLOTS, width // 2 + LANES), BF),
            pltpu.VMEM((width, 2 * ff), BF),
            pltpu.VMEM((2, quarter_g, 2 * ff), BF),
            pltpu.VMEM((2, quarter_d, width), BF),
            pltpu.VMEM((2 * (GZ - 1) * tok_rows, width), BF),
            pltpu.VMEM((GZ, SLOTS, tok_rows), F32),
            pltpu.VMEM((rows // CHUNKS * (CHUNKS - 1), 2 * ff), F32),
            dma((2 * GZ - 2,)), dma((2 * GZ - 2,)), dma, dma,
            dma, dma((CHUNKS,)), dma, dma,
            dma((pieces,)), dma((pieces,)), dma((pieces,)), dma((pieces,)),
            dma((pieces,)), dma((pieces,)), dma((pieces,)), dma((pieces,)),
            dma((4,)), dma((4,)), dma((2,)), dma((2,)),
        ],
        compiler_params=pltpu.CompilerParams(
            has_side_effects=True, vmem_limit_bytes=VMEM_BYTES
        ),
        cost_estimate=pl.CostEstimate(
            flops=flops, bytes_accessed=12 * 2**20, transcendentals=rows * ff
        ),
    )(
        routes.T, slot_index.T, route_weight.T, swap_flags[None], tokens, cotangent, w_gate_up[0], w_down[0]
    )

    grad_tokens, grad_weight, grad_gu, grad_dn = pl.pallas_call(
        finish_kernel,
        name="finish",
        out_shape=(
            jax.ShapeDtypeStruct((tok_rows, width), F32),
            jax.ShapeDtypeStruct((3, tok_rows), F32),
            jax.ShapeDtypeStruct((quarter_g, 2 * ff), F32),
            jax.ShapeDtypeStruct((quarter_d, width), F32),
        ),
        in_specs=[hbm] * 5 + [vmem] * 4,
        out_specs=(hbm, vmem, hbm, hbm),
        scratch_shapes=[
            pltpu.VMEM(ret.shape, BF),
            pltpu.VMEM((quarter_g, 2 * ff), BF),
            pltpu.VMEM((quarter_g, 2 * ff), BF),
            pltpu.VMEM((quarter_d, width), BF),
            pltpu.VMEM((quarter_d, width), BF),
            pltpu.VMEM((quarter_g, 2 * ff), F32),
            pltpu.VMEM((quarter_d, width), F32),
            pltpu.VMEM((tok_rows, width), F32),
            dma((17,)),
            dma((9,)),
        ],
        compiler_params=pltpu.CompilerParams(vmem_limit_bytes=VMEM_BYTES),
    )(
        ret, own_g, own_d, far_g, far_d,
        routes.T, slot_index.T, route_weight.T, swap_flags[None],
    )
    return (grad_tokens, grad_weight.T, grad_gu[None], grad_dn[None])


def solution(mesh):
    return jax.shard_map(
        functools.partial(body, 'DWCGRS'),
        mesh=mesh,
        in_specs=(
            P(("dp", "expert"), None),
            P(("dp", "expert"), None),
            P(("dp", "expert"), None),
            P(("dp", "expert"), None),
            P(("dp", "expert"), None),
            P(),
            P("expert", "dp", None),
            P("expert", "dp", None),
        ),
        out_specs=(
            P(("dp", "expert"), None),
            P(("dp", "expert"), None),
            P("expert", "dp", None),
            P("expert", "dp", None),
        ),
        check_vma=False,
    )
```

```python
import functools

import jax
import jax.numpy as jnp
from jax import lax
from jax.experimental import pallas as pl
from jax.experimental.pallas import tpu as pltpu
from jax.sharding import PartitionSpec as P

BF = jnp.bfloat16
F32 = jnp.float32
MESH = pl.DeviceIdType.MESH
GX, GZ, GY = 4, 8, 2
CHUNKS = 4
PIECES_G, PIECES_D = 8, 4
AHEAD, FIRST = 12, 6
DEFER = 0
SLOTS = 8
LANES = 128
VMEM_BYTES = 61 * 2**20

ROWS_BY_ROWS = (((1,), (1,)), ((), ()))
COLS_BY_COLS = (((0,), (0,)), ((), ()))


def pick_tile(width, largest):
    tile = min(width, largest)
    while width % tile:
        tile -= LANES
    return tile


def offsets_of(i):
    place, code = i // (GX * GY), i % (GX * GY)
    odd = place % 2
    dz = odd * ((place + 1) // 2) + (1 - odd) * ((GZ - place // 2) % GZ)
    return code // GY, dz, code % GY


def shifted(me, dx, dz, dy):
    x, z, y = me // (GZ * GY), (me // GY) % GZ, me % GY
    return ((x + dx) % GX) * (GZ * GY) + ((z + dz) % GZ) * GY + (y + dy) % GY


def partner(me, i, sign):
    dx, dz, dy = offsets_of(i)
    if sign < 0:
        dx, dz = GX - dx, GZ - dz
    return shifted(me, dx, dz, dy)


def replica(dp, i):
    crosses = (i % GY) * (dp % 2)
    return dp + crosses * (2 - 4 * (dp // 2))


def codes_of(me, first, rows, dim, flag_ref):
    experts = flag_ref.shape[1]
    if dim == 0:
        row = first + lax.broadcasted_iota(jnp.int32, (rows, experts), 0)
        slot = shifted(me, row // (SLOTS * GY), 0, (row // SLOTS) % GY)
        lane = lax.broadcasted_iota(jnp.int32, (rows, experts), 1)
        hit = jnp.where(lane == slot, 1.0, 0.0) * flag_ref[...].astype(F32)
        moved = jnp.max(hit, axis=1, keepdims=True)
        row, slot = row[:, :1], slot[:, :1]
    else:
        row = first + lax.broadcasted_iota(jnp.int32, (experts, rows), 1)
        slot = partner(me, row // SLOTS, 1)
        line = lax.broadcasted_iota(jnp.int32, (experts, rows), 0)
        hit = jnp.where(line == slot, 1.0, 0.0).astype(BF)
        flags = jnp.broadcast_to(flag_ref[...].astype(F32), (16, experts)).astype(BF)
        moved = jnp.dot(flags, hit, preferred_element_type=F32)[:1, :]
        row, slot = row[:1, :], slot[:1, :]
    home = jnp.where(moved > 0.5, slot ^ (experts // 2), slot)
    return home * SLOTS + row % SLOTS


def exchange_kernel(
    parts, sizes, route_ref, slot_ref, weight_ref, flag_ref, tok_ref, cot_ref, wg_ref, wd_ref,
    ret_ref, own_g, own_d, far_g, far_d,
    sendb, recvb, mig_g, mig_d, full_g, full_d, rows_b, scaled_b, hid_b, both_b,
    retb, part_g, sib_g, sib_d, gathered, meta, gate_up,
    ring_send, ring_recv, meta_send, meta_recv, a2a_send, a2a_recv, ret_send, ret_recv,
    mig_send, mig_recv, far_send, far_recv, sib_send, sib_recv, fwd_send, fwd_recv,
    red_send, red_recv, out_send, out_recv,
):
    experts, width, ff = sizes
    block = experts // CHUNKS
    chunk = block * SLOTS
    half = width // 2
    quarter_g, quarter_d = width // 4, ff // 4
    tokens = tok_ref.shape[0]
    dp = lax.axis_index("dp")
    me = lax.axis_index("expert")
    sib, far = dp ^ 1, dp ^ 2

    def remote(src, dst, send, recv, where):
        return pltpu.make_async_remote_copy(
            src_ref=src, dst_ref=dst, send_sem=send, recv_sem=recv,
            device_id=where, device_id_type=MESH,
        )

    step_g, step_d = quarter_g // PIECES_G, quarter_d // PIECES_D
    pieces = [(True, k * step_g, step_g) for k in range(PIECES_G)]
    pieces += [(False, k * step_d, step_d) for k in range(PIECES_D)]
    if "W" not in parts:
        pieces = []
    swaps, fars, sibs, fwds = [], [], [], []

    def swap(k):
        if k >= len(pieces):
            return
        is_g, off, count = pieces[k]
        src, dst = (wg_ref, mig_g) if is_g else (wd_ref, mig_d)
        rows = pl.ds(off, count)
        copy = remote(
            src.at[rows], dst.at[rows], mig_send.at[k], mig_recv.at[k], (dp, me ^ (experts // 2))
        )
        copy.start()
        swaps.append(copy)

    def gather(k):
        is_g, off, count = pieces[k]
        if is_g:
            own, mig, full, quarter = wg_ref, mig_g, full_g, quarter_g
        else:
            own, mig, full, quarter = wd_ref, mig_d, full_d, quarter_d
        swaps[k].wait_recv()
        rows = pl.ds(off, count)
        place = pl.ds(pl.multiple_of(dp * quarter + off, 16), count)
        full[place, :] = jnp.where(flagged, mig[rows, :], own[rows, :])
        copy = remote(full.at[place], full.at[place], far_send.at[k], far_recv.at[k], (far, me))
        copy.start()
        fars.append(copy)
        copy = remote(full.at[place], full.at[place], sib_send.at[k], sib_recv.at[k], (sib, me))
        copy.start()
        sibs.append(copy)

    def forward(k):
        is_g, off, count = pieces[k]
        full, quarter = (full_g, quarter_g) if is_g else (full_d, quarter_d)
        fars[k].wait_recv()
        place = pl.ds(pl.multiple_of(far * quarter + off, 16), count)
        copy = remote(full.at[place], full.at[place], fwd_send.at[k], fwd_recv.at[k], (sib, me))
        copy.start()
        fwds.append(copy)

    prep_tile = pick_tile(width, 512)
    plane = GX * GY
    picked = plane * SLOTS

    def rows_at(dz, part):
        return pl.ds((2 * (dz - 1) + part) * tokens, tokens)

    def block_at(dz, part):
        return gathered.at[rows_at(dz, part)]

    def hop(src, dz, part, way):
        where = (dp, shifted(me, 0, way % GZ, 0))
        k = 2 * (dz - 1) + part
        copy = remote(src, block_at(dz, part), ring_send.at[k], ring_recv.at[k], where)
        copy.start()
        hops.append(copy)

    def landed(dz, part):
        k = 2 * (dz - 1) + part
        here = block_at(dz, part)
        pltpu.make_async_copy(here, here, ring_recv.at[k]).wait()
        if dz < GZ // 2 - 1 or (dz == GZ // 2 - 1 and part == 0):
            hop(here, dz + 1, part, 1)
        if dz > GZ // 2 + 1 or (dz == GZ // 2 + 1 and part == 1):
            hop(here, dz - 1, part, -1)

    def prepare(place):
        dz = offsets_of(place * plane)[1]
        pick = jnp.zeros((picked, tokens), F32)
        pick_w = jnp.zeros((picked, tokens), F32)
        for k in range(3):
            hit = codes == meta[dz, k : k + 1, :]
            pick = jnp.where(hit, 1.0, pick)
            pick_w = jnp.where(hit, meta[dz, 4 + k : 5 + k, :], pick_w)
        pick = pick.astype(BF)
        pick_w = pick_w.astype(BF)
        first = place * plane
        for col in range(0, width, prep_tile):
            cols = slice(col, col + prep_tile)
            tok = tok_ref[:, cols] if dz == 0 else gathered[rows_at(dz, 0), cols]
            cot = cot_ref[:, cols] if dz == 0 else gathered[rows_at(dz, 1), cols]
            rows = jnp.dot(pick, tok, preferred_element_type=F32)
            cots = jnp.dot(pick_w, cot, preferred_element_type=F32)
            both = jnp.concatenate(
                [rows.reshape(plane, SLOTS, prep_tile), cots.reshape(plane, SLOTS, prep_tile)],
                axis=1,
            )
            sendb[first : first + plane, :, cols] = both.astype(BF)

    def push(place):
        first = place * plane
        chunk_sem = a2a_recv.at[first // block]
        pltpu.make_async_copy(sendb.at[first], recvb.at[first], chunk_sem).start()

        def send(j, carry):
            where = (replica(dp, j), shifted(me, j // GY, 0, j % GY))
            i = first + j
            remote(sendb.at[i], recvb.at[i], a2a_send, chunk_sem, where).start()
            return carry

        lax.fori_loop(1, plane, send, 0)

    for k in range(AHEAD):
        swap(k)
    hops = []
    if "D" in parts:
        meta[0] = jnp.zeros((SLOTS, tokens), F32)
        for k in range(3):
            code = route_ref[k : k + 1, :] * SLOTS + slot_ref[k : k + 1, :]
            meta[0, k : k + 1, :] = code.astype(F32)
            meta[0, 4 + k : 5 + k, :] = weight_ref[k : k + 1, :].astype(BF).astype(F32)
        for part, src in ((0, tok_ref), (1, cot_ref)):
            hop(src, 1, part, 1)
            hop(src, GZ - 1, part, -1)

        def send_meta(dz, carry):
            where = (dp, shifted(me, 0, dz, 0))
            remote(meta.at[0], meta.at[dz], meta_send, meta_recv, where).start()
            return carry

        lax.fori_loop(1, GZ, send_meta, 0)
        codes = codes_of(me, 0, picked, 0, flag_ref).astype(F32)
    lane = lax.broadcasted_iota(jnp.int32, flag_ref.shape, 1)
    mine = jnp.where(lane == me, flag_ref[...], 0).astype(F32)
    flagged = jnp.max(mine, axis=1, keepdims=True) > 0.5

    ff_tile = pick_tile(ff, 256)
    half_tile = pick_tile(half, 256)

    def forward_part(first, count):
        rows_n = count * SLOTS
        place = pl.ds(first * SLOTS, rows_n)
        for col in range(0, width, prep_tile):
            cols = slice(col, col + prep_tile)
            both = recvb[first : first + count, :, cols].astype(F32)
            rows_b[place, cols] = both[:, :SLOTS].reshape(rows_n, prep_tile).astype(BF)
            scaled_b[place, cols] = both[:, SLOTS:].reshape(rows_n, prep_tile).astype(BF)
        for f in range(0, 2 * ff, ff_tile):
            cols = slice(f, f + ff_tile)
            gate_up[:rows_n, cols] = jnp.dot(
                rows_b[place, :], full_g[:, cols], preferred_element_type=F32
            )

    def backward_part(first, count):
        rows_n = count * SLOTS
        place = pl.ds(first * SLOTS, rows_n)
        prob = jnp.zeros((rows_n, 1), F32)
        for f in range(0, ff, ff_tile):
            cols = slice(f, f + ff_tile)
            up_cols = slice(ff + f, ff + f + ff_tile)
            gate, up = gate_up[:rows_n, cols], gate_up[:rows_n, up_cols]
            hgrad = lax.dot_general(
                scaled_b[place, :], full_d[cols, :], ROWS_BY_ROWS, preferred_element_type=F32
            )
            sig = jax.nn.sigmoid(gate)
            silu = gate * sig
            hid = (silu * up).astype(BF)
            hid_b[place, cols] = hid
            both_b[place, cols] = (hgrad * up * sig * (1.0 + gate * (1.0 - sig))).astype(BF)
            both_b[place, up_cols] = (hgrad * silu).astype(BF)
            prob = prob + jnp.sum(hid.astype(F32) * hgrad, axis=1, keepdims=True)
        prob = jnp.broadcast_to(prob, (rows_n, LANES))
        rough = prob.astype(BF).astype(F32)
        both = jnp.concatenate(
            [rough.reshape(count, SLOTS, LANES), (prob - rough).reshape(count, SLOTS, LANES)],
            axis=1,
        )
        retb[first : first + count, :, half : half + LANES] = both.astype(BF)

    def row_grads(first, count):
        place = pl.ds(first * SLOTS, count * SLOTS)
        for col in range(0, half, half_tile):
            lo = lax.dot_general(
                both_b[place, :], full_g[col : col + half_tile, :], ROWS_BY_ROWS,
                preferred_element_type=F32,
            )
            hi = lax.dot_general(
                both_b[place, :], full_g[half + col : half + col + half_tile, :], ROWS_BY_ROWS,
                preferred_element_type=F32,
            )
            both = jnp.concatenate(
                [lo.reshape(count, SLOTS, half_tile), hi.reshape(count, SLOTS, half_tile)], axis=1
            )
            retb[first : first + count, :, col : col + half_tile] = both.astype(BF)

    def give_back(c):
        if "R" not in parts:
            return

        def send(j, carry):
            i = c * block + j

            @pl.when(i > 0)
            def _():
                remote(
                    retb.at[i], ret_ref.at[i], ret_send, ret_recv,
                    (replica(dp, i), partner(me, i, -1)),
                ).start()

            return carry

        lax.fori_loop(0, block, send, 0)

    def arrive(c):
        if "D" in parts:
            arrived = recvb.at[pl.ds(c * block, block)]
            pltpu.make_async_copy(arrived, arrived, a2a_recv.at[c]).wait()

    def weights(gathers, forwards):
        for k in gathers:
            if k < len(pieces):
                gather(k)
                swap(k + AHEAD)
        for k in forwards:
            if k < len(pieces):
                forward(k)

    total = PIECES_G + PIECES_D
    plan = {
        1: (range(FIRST), ()),
        2: (range(FIRST, total), range(FIRST)),
        3: ((), range(FIRST, total)),
    }
    if "D" in parts:
        prepare(0)
        if DEFER == 0:
            push(0)
        others = meta.at[pl.ds(1, GZ - 1)]
        pltpu.make_async_copy(others, others, meta_recv).wait()
    for t in range(1, GZ // 2):
        if "D" in parts:
            for part in range(2):
                landed(t, part)
                landed(GZ - t, part)
        if t <= DEFER:
            weights(*plan[t])
        if "D" in parts:
            for place in (2 * t - 1, 2 * t):
                prepare(place)
                if t > DEFER:
                    push(place)
            if t == DEFER:
                for place in range(2 * t + 1):
                    push(place)
        if t > DEFER:
            weights(*plan[t])
    if "D" in parts:
        for part in range(2):
            landed(GZ // 2, part)
        prepare(GZ - 1)
        push(GZ - 1)

    def complete(first, stop):
        for k in range(first, min(stop, len(pieces))):
            sibs[k].wait_recv()
            fwds[k].wait_recv()

    last = CHUNKS - 1
    ahead = last * block
    for c in range(last):
        arrive(c)
    complete(0, PIECES_G)
    if "C" in parts:
        forward_part(0, ahead)
    complete(PIECES_G, total)
    if "C" in parts:
        backward_part(0, ahead)
        row_grads(0, ahead)
    if "R" in parts:
        pltpu.make_async_copy(retb.at[0], ret_ref.at[0], ret_recv).start()
    for c in range(last):
        give_back(c)
    arrive(last)
    if "C" in parts:
        forward_part(ahead, block)
        backward_part(ahead, block)

    wide = pick_tile(2 * ff, 768)
    d_tile = pick_tile(quarter_g, 256)

    def gate_up_grads(quarter, i):
        if "G" not in parts:
            return
        start = pl.multiple_of(quarter * quarter_g + i * d_tile, d_tile)
        left = rows_b[:, pl.ds(start, d_tile)]
        for c in range(0, 2 * ff, wide):
            part_g[pl.ds(start, d_tile), c : c + wide] = lax.dot_general(
                left, both_b[:, c : c + wide], COLS_BY_COLS, preferred_element_type=F32
            ).astype(BF)

    part_d = gathered

    def down_grads():
        for copy in hops:
            copy.wait_send()
        if "G" not in parts:
            return
        for f in range(0, ff, ff_tile):
            for c in range(0, width, prep_tile):
                part_d[f : f + ff_tile, c : c + prep_tile] = lax.dot_general(
                    hid_b[:, f : f + ff_tile], scaled_b[:, c : c + prep_tile], COLS_BY_COLS,
                    preferred_element_type=F32,
                ).astype(BF)

    def place_of(quarter, rows):
        return pl.ds(pl.multiple_of(quarter * rows, 16), rows)

    reds = []

    def to_sibling(slot, part, rows, landing, quarter, where, off, count):
        copy = remote(
            part.at[pl.ds(pl.multiple_of(quarter * rows + off, 16), count)],
            landing.at[where, pl.ds(off, count)],
            red_send.at[slot], red_recv.at[slot], (sib, me),
        )
        copy.start()
        reds.append(copy)

    outs = []

    def to_far(slot, part, rows, landing, out, off, count):
        reds[slot].wait_recv()
        mine = part[pl.ds(pl.multiple_of(far * rows + off, 16), count), :].astype(F32)
        place = pl.ds(off, count)
        landing[0, place, :] = (mine + landing[0, place, :].astype(F32)).astype(BF)
        copy = remote(
            landing.at[0, place], out.at[place], out_send.at[slot], out_recv.at[slot], (far, me)
        )
        copy.start()
        outs.append(copy)

    tiles = quarter_g // d_tile
    for i in range(tiles):
        gate_up_grads(far ^ 1, i)
        to_sibling(i, part_g, quarter_g, sib_g, far ^ 1, 0, i * d_tile, d_tile)
    for i in range(tiles):
        gate_up_grads(far, i)
        if i > 0:
            to_far(i - 1, part_g, quarter_g, sib_g, far_g, (i - 1) * d_tile, d_tile)
    to_far(tiles - 1, part_g, quarter_g, sib_g, far_g, (tiles - 1) * d_tile, d_tile)
    if "C" in parts:
        row_grads(ahead, block)
    give_back(last)
    down_grads()
    to_sibling(tiles, part_d, quarter_d, sib_d, far ^ 1, 0, 0, quarter_d)
    to_sibling(tiles + 1, part_d, quarter_d, sib_d, dp ^ 1, 1, 0, quarter_d)
    for i in range(tiles):
        gate_up_grads(dp ^ 1, i)
    to_sibling(tiles + 2, part_g, quarter_g, sib_g, dp ^ 1, 1, 0, quarter_g)
    to_far(tiles, part_d, quarter_d, sib_d, far_d, 0, quarter_d)
    for i in range(tiles):
        gate_up_grads(dp, i)
    if "S" in parts:
        reds[tiles + 1].wait_recv()
        own_d[...] = (
            part_d[place_of(dp, quarter_d), :].astype(F32) + sib_d[1].astype(F32)
        ).astype(BF)
        reds[tiles + 2].wait_recv()
        own_g[...] = (
            part_g[place_of(dp, quarter_g), :].astype(F32) + sib_g[1].astype(F32)
        ).astype(BF)

    if "D" in parts:
        others = sendb.at[pl.ds(0, experts - GZ)]
        pltpu.make_async_copy(others, others, a2a_send).wait()
        others = meta.at[pl.ds(1, GZ - 1)]
        pltpu.make_async_copy(others, others, meta_send).wait()
    for copy in swaps + fars + sibs + fwds + reds:
        copy.wait_send()
    if "R" in parts:
        others = retb.at[pl.ds(1, experts - 1)]
        pltpu.make_async_copy(others, others, ret_send).wait()
        pltpu.make_async_copy(retb, retb, ret_recv).wait()
    for copy in outs:
        copy.wait()


def finish_kernel(
    ret_hbm, own_g, own_d, far_g, far_d, route_ref, slot_ref, weight_ref, flag_ref,
    tok_out, weight_out, out_g, out_d,
    ret_ref, a_g, b_g, a_d, b_d, sum_g, sum_d, tok_ref, in_sem, out_sem,
):
    experts, _, cols = ret_ref.shape
    half = cols - LANES
    rows = experts * SLOTS
    load_ret = pltpu.make_async_copy(ret_hbm, ret_ref, in_sem.at[0])
    load_ret.start()
    steps = 4
    step_g, step_d = a_g.shape[0] // steps, a_d.shape[0] // steps
    loads = []
    for k in range(steps):
        for n, (src, dst, step) in enumerate(
            ((own_g, a_g, step_g), (far_g, b_g, step_g), (own_d, a_d, step_d), (far_d, b_d, step_d))
        ):
            part = pl.ds(k * step, step)
            copy = pltpu.make_async_copy(src.at[part], dst.at[part], in_sem.at[1 + 4 * k + n])
            copy.start()
            loads.append(copy)
    codes = codes_of(lax.axis_index("expert"), 0, rows, 1, flag_ref)
    tokens = route_ref.shape[1]
    hits = []
    for k in range(3):
        code = (route_ref[k : k + 1, :] * SLOTS + slot_ref[k : k + 1, :]).astype(F32)
        hits.append(codes == jnp.broadcast_to(code, (LANES, tokens)).T[:, :1].astype(jnp.int32))
    pick = jnp.zeros(hits[0].shape, F32)
    for hit in hits:
        pick = jnp.where(hit, 1.0, pick)
    pick = pick.astype(BF)
    load_ret.wait()
    stores = []

    def store(src, dst, n):
        copy = pltpu.make_async_copy(src, dst, out_sem.at[n])
        copy.start()
        stores.append(copy)

    tile = pick_tile(half, 512)
    for c in range(0, half, tile):
        both = ret_ref[:, :, c : c + tile].astype(F32)
        lo = both[:, :SLOTS].reshape(rows, tile).astype(BF)
        hi = both[:, SLOTS:].reshape(rows, tile).astype(BF)
        tok_ref[:, c : c + tile] = jnp.dot(pick, lo, preferred_element_type=F32)
        tok_ref[:, half + c : half + c + tile] = jnp.dot(pick, hi, preferred_element_type=F32)
    store(tok_ref, tok_out, 0)
    for k in range(steps):
        for copy in loads[4 * k : 4 * k + 4]:
            copy.wait()
        part = pl.ds(k * step_g, step_g)
        sum_g[part, :] = a_g[part, :].astype(F32) + b_g[part, :].astype(F32)
        store(sum_g.at[part], out_g.at[part], 1 + 2 * k)
        part = pl.ds(k * step_d, step_d)
        sum_d[part, :] = a_d[part, :].astype(F32) + b_d[part, :].astype(F32)
        store(sum_d.at[part], out_d.at[part], 2 + 2 * k)
    both = ret_ref[:, :, half:].astype(F32)
    rough = both[:, :SLOTS].reshape(rows, LANES).astype(BF)
    rest = both[:, SLOTS:].reshape(rows, LANES).astype(BF)
    for k in range(3):
        one = jnp.where(hits[k], 1.0, 0.0).astype(BF)
        prob = jnp.dot(one, rough, preferred_element_type=F32)
        prob = prob + jnp.dot(one, rest, preferred_element_type=F32)
        weight_out[k : k + 1, :] = prob.T[:1, :] / weight_ref[k : k + 1, :].astype(BF).astype(F32)
    for copy in stores:
        copy.wait()


def body(parts, tokens, cotangent, routes, slot_index, route_weight, swap_flags, w_gate_up, w_down):
    tok_rows, width = tokens.shape
    experts = swap_flags.shape[0]
    ff = w_down.shape[1] * lax.axis_size("dp")
    rows = experts * SLOTS
    quarter_g, quarter_d = w_gate_up.shape[1], w_down.shape[1]
    pieces = PIECES_G + PIECES_D

    vmem = pl.BlockSpec(memory_space=pltpu.VMEM)
    hbm = pl.BlockSpec(memory_space=pl.ANY)
    dma = pltpu.SemaphoreType.DMA
    flops = 2 * rows * width * ff * 9
    ret, own_g, own_d, far_g, far_d = pl.pallas_call(
        functools.partial(exchange_kernel, parts, (experts, width, ff)),
        name="ex_" + "".join(parts),
        out_shape=(
            jax.ShapeDtypeStruct((experts, 2 * SLOTS, width // 2 + LANES), BF),
            jax.ShapeDtypeStruct((quarter_g, 2 * ff), BF),
            jax.ShapeDtypeStruct((quarter_d, width), BF),
            jax.ShapeDtypeStruct((quarter_g, 2 * ff), BF),
            jax.ShapeDtypeStruct((quarter_d, width), BF),
        ),
        in_specs=[vmem] * 8,
        out_specs=(hbm, vmem, vmem, hbm, hbm),
        scratch_shapes=[
            pltpu.VMEM((experts, 2 * SLOTS, width), BF),
            pltpu.VMEM((experts, 2 * SLOTS, width), BF),
            pltpu.VMEM((quarter_g, 2 * ff), BF),
            pltpu.VMEM((quarter_d, width), BF),
            pltpu.VMEM((width, 2 * ff), BF),
            pltpu.VMEM((ff, width), BF),
            pltpu.VMEM((rows, width), BF),
            pltpu.VMEM((rows, width), BF),
            pltpu.VMEM((rows, ff), BF),
            pltpu.VMEM((rows, 2 * ff), BF),
            pltpu.VMEM((experts, 2 * SLOTS, width // 2 + LANES), BF),
            pltpu.VMEM((width, 2 * ff), BF),
            pltpu.VMEM((2, quarter_g, 2 * ff), BF),
            pltpu.VMEM((2, quarter_d, width), BF),
            pltpu.VMEM((2 * (GZ - 1) * tok_rows, width), BF),
            pltpu.VMEM((GZ, SLOTS, tok_rows), F32),
            pltpu.VMEM((rows // CHUNKS * (CHUNKS - 1), 2 * ff), F32),
            dma((2 * GZ - 2,)), dma((2 * GZ - 2,)), dma, dma,
            dma, dma((CHUNKS,)), dma, dma,
            dma((pieces,)), dma((pieces,)), dma((pieces,)), dma((pieces,)),
            dma((pieces,)), dma((pieces,)), dma((pieces,)), dma((pieces,)),
            dma((8,)), dma((8,)), dma((4,)), dma((4,)),
        ],
        compiler_params=pltpu.CompilerParams(
            has_side_effects=True, vmem_limit_bytes=VMEM_BYTES
        ),
        cost_estimate=pl.CostEstimate(
            flops=flops, bytes_accessed=12 * 2**20, transcendentals=rows * ff
        ),
    )(
        routes.T, slot_index.T, route_weight.T, swap_flags[None], tokens, cotangent, w_gate_up[0], w_down[0]
    )

    grad_tokens, grad_weight, grad_gu, grad_dn = pl.pallas_call(
        finish_kernel,
        name="finish",
        out_shape=(
            jax.ShapeDtypeStruct((tok_rows, width), F32),
            jax.ShapeDtypeStruct((3, tok_rows), F32),
            jax.ShapeDtypeStruct((quarter_g, 2 * ff), F32),
            jax.ShapeDtypeStruct((quarter_d, width), F32),
        ),
        in_specs=[hbm] * 5 + [vmem] * 4,
        out_specs=(hbm, vmem, hbm, hbm),
        scratch_shapes=[
            pltpu.VMEM(ret.shape, BF),
            pltpu.VMEM((quarter_g, 2 * ff), BF),
            pltpu.VMEM((quarter_g, 2 * ff), BF),
            pltpu.VMEM((quarter_d, width), BF),
            pltpu.VMEM((quarter_d, width), BF),
            pltpu.VMEM((quarter_g, 2 * ff), F32),
            pltpu.VMEM((quarter_d, width), F32),
            pltpu.VMEM((tok_rows, width), F32),
            dma((17,)),
            dma((9,)),
        ],
        compiler_params=pltpu.CompilerParams(vmem_limit_bytes=VMEM_BYTES),
    )(
        ret, own_g, own_d, far_g, far_d,
        routes.T, slot_index.T, route_weight.T, swap_flags[None],
    )
    return (grad_tokens, grad_weight.T, grad_gu[None], grad_dn[None])


def solution(mesh):
    return jax.shard_map(
        functools.partial(body, 'DWCGRS'),
        mesh=mesh,
        in_specs=(
            P(("dp", "expert"), None),
            P(("dp", "expert"), None),
            P(("dp", "expert"), None),
            P(("dp", "expert"), None),
            P(("dp", "expert"), None),
            P(),
            P("expert", "dp", None),
            P("expert", "dp", None),
        ),
        out_specs=(
            P(("dp", "expert"), None),
            P(("dp", "expert"), None),
            P("expert", "dp", None),
            P("expert", "dp", None),
        ),
        check_vma=False,
    )
```

```python
import functools

import jax
import jax.numpy as jnp
from jax import lax
from jax.experimental import pallas as pl
from jax.experimental.pallas import tpu as pltpu
from jax.sharding import PartitionSpec as P

BF = jnp.bfloat16
F32 = jnp.float32
MESH = pl.DeviceIdType.MESH
GX, GZ, GY = 4, 8, 2
CHUNKS = 4
PIECES_G, PIECES_D = 8, 4
AHEAD, FIRST = 12, 6
DEFER = 0
SLOTS = 8
LANES = 128
VMEM_BYTES = 61 * 2**20

ROWS_BY_ROWS = (((1,), (1,)), ((), ()))
COLS_BY_COLS = (((0,), (0,)), ((), ()))


def pick_tile(width, largest):
    tile = min(width, largest)
    while width % tile:
        tile -= LANES
    return tile


def offsets_of(i):
    place, code = i // (GX * GY), i % (GX * GY)
    odd = place % 2
    dz = odd * ((place + 1) // 2) + (1 - odd) * ((GZ - place // 2) % GZ)
    return code // GY, dz, code % GY


def shifted(me, dx, dz, dy):
    x, z, y = me // (GZ * GY), (me // GY) % GZ, me % GY
    return ((x + dx) % GX) * (GZ * GY) + ((z + dz) % GZ) * GY + (y + dy) % GY


def partner(me, i, sign):
    dx, dz, dy = offsets_of(i)
    if sign < 0:
        dx, dz = GX - dx, GZ - dz
    return shifted(me, dx, dz, dy)


def replica(dp, i):
    crosses = (i % GY) * (dp % 2)
    return dp + crosses * (2 - 4 * (dp // 2))


def codes_of(me, first, rows, dim, flag_ref):
    experts = flag_ref.shape[1]
    if dim == 0:
        row = first + lax.broadcasted_iota(jnp.int32, (rows, experts), 0)
        slot = shifted(me, row // (SLOTS * GY), 0, (row // SLOTS) % GY)
        lane = lax.broadcasted_iota(jnp.int32, (rows, experts), 1)
        hit = jnp.where(lane == slot, 1.0, 0.0) * flag_ref[...].astype(F32)
        moved = jnp.max(hit, axis=1, keepdims=True)
        row, slot = row[:, :1], slot[:, :1]
    else:
        row = first + lax.broadcasted_iota(jnp.int32, (experts, rows), 1)
        slot = partner(me, row // SLOTS, 1)
        line = lax.broadcasted_iota(jnp.int32, (experts, rows), 0)
        hit = jnp.where(line == slot, 1.0, 0.0).astype(BF)
        flags = jnp.broadcast_to(flag_ref[...].astype(F32), (16, experts)).astype(BF)
        moved = jnp.dot(flags, hit, preferred_element_type=F32)[:1, :]
        row, slot = row[:1, :], slot[:1, :]
    home = jnp.where(moved > 0.5, slot ^ (experts // 2), slot)
    return home * SLOTS + row % SLOTS


def exchange_kernel(
    parts, sizes, route_ref, slot_ref, weight_ref, flag_ref, tok_ref, cot_ref, wg_ref, wd_ref,
    ret_ref, own_g, own_d, far_g, far_d,
    sendb, recvb, mig_g, mig_d, full_g, full_d, rows_b, scaled_b, hid_b, both_b,
    retb, part_g, sib_g, sib_d, gathered, meta, gate_up,
    ring_send, ring_recv, meta_send, meta_recv, a2a_send, a2a_recv, ret_send, ret_recv,
    mig_send, mig_recv, far_send, far_recv, sib_send, sib_recv, fwd_send, fwd_recv,
    red_send, red_recv, out_send, out_recv,
):
    experts, width, ff = sizes
    block = experts // CHUNKS
    chunk = block * SLOTS
    half = width // 2
    quarter_g, quarter_d = width // 4, ff // 4
    tokens = tok_ref.shape[0]
    dp = lax.axis_index("dp")
    me = lax.axis_index("expert")
    sib, far = dp ^ 1, dp ^ 2

    def remote(src, dst, send, recv, where):
        return pltpu.make_async_remote_copy(
            src_ref=src, dst_ref=dst, send_sem=send, recv_sem=recv,
            device_id=where, device_id_type=MESH,
        )

    step_g, step_d = quarter_g // PIECES_G, quarter_d // PIECES_D
    pieces = [(True, k * step_g, step_g) for k in range(PIECES_G)]
    pieces += [(False, k * step_d, step_d) for k in range(PIECES_D)]
    if "W" not in parts:
        pieces = []
    swaps, fars, sibs, fwds = [], [], [], []

    def swap(k):
        if k >= len(pieces):
            return
        is_g, off, count = pieces[k]
        src, dst = (wg_ref, mig_g) if is_g else (wd_ref, mig_d)
        rows = pl.ds(off, count)
        copy = remote(
            src.at[rows], dst.at[rows], mig_send.at[k], mig_recv.at[k], (dp, me ^ (experts // 2))
        )
        copy.start()
        swaps.append(copy)

    def gather(k):
        is_g, off, count = pieces[k]
        if is_g:
            own, mig, full, quarter = wg_ref, mig_g, full_g, quarter_g
        else:
            own, mig, full, quarter = wd_ref, mig_d, full_d, quarter_d
        swaps[k].wait_recv()
        rows = pl.ds(off, count)
        place = pl.ds(pl.multiple_of(dp * quarter + off, 16), count)
        full[place, :] = jnp.where(flagged, mig[rows, :], own[rows, :])
        copy = remote(full.at[place], full.at[place], far_send.at[k], far_recv.at[k], (far, me))
        copy.start()
        fars.append(copy)
        copy = remote(full.at[place], full.at[place], sib_send.at[k], sib_recv.at[k], (sib, me))
        copy.start()
        sibs.append(copy)

    def forward(k):
        is_g, off, count = pieces[k]
        full, quarter = (full_g, quarter_g) if is_g else (full_d, quarter_d)
        fars[k].wait_recv()
        place = pl.ds(pl.multiple_of(far * quarter + off, 16), count)
        copy = remote(full.at[place], full.at[place], fwd_send.at[k], fwd_recv.at[k], (sib, me))
        copy.start()
        fwds.append(copy)

    prep_tile = pick_tile(width, 512)
    plane = GX * GY
    picked = plane * SLOTS

    def rows_at(dz, part):
        return pl.ds((2 * (dz - 1) + part) * tokens, tokens)

    def block_at(dz, part):
        return gathered.at[rows_at(dz, part)]

    def hop(src, dz, part, way):
        where = (dp, shifted(me, 0, way % GZ, 0))
        k = 2 * (dz - 1) + part
        copy = remote(src, block_at(dz, part), ring_send.at[k], ring_recv.at[k], where)
        copy.start()
        hops.append(copy)

    def landed(dz, part):
        k = 2 * (dz - 1) + part
        here = block_at(dz, part)
        pltpu.make_async_copy(here, here, ring_recv.at[k]).wait()
        if dz < GZ // 2 - 1 or (dz == GZ // 2 - 1 and part == 0):
            hop(here, dz + 1, part, 1)
        if dz > GZ // 2 + 1 or (dz == GZ // 2 + 1 and part == 1):
            hop(here, dz - 1, part, -1)

    def prepare(place):
        dz = offsets_of(place * plane)[1]
        pick = jnp.zeros((picked, tokens), F32)
        pick_w = jnp.zeros((picked, tokens), F32)
        for k in range(3):
            hit = codes == meta[dz, k : k + 1, :]
            pick = jnp.where(hit, 1.0, pick)
            pick_w = jnp.where(hit, meta[dz, 4 + k : 5 + k, :], pick_w)
        pick = pick.astype(BF)
        pick_w = pick_w.astype(BF)
        first = place * plane
        for col in range(0, width, prep_tile):
            cols = slice(col, col + prep_tile)
            tok = tok_ref[:, cols] if dz == 0 else gathered[rows_at(dz, 0), cols]
            cot = cot_ref[:, cols] if dz == 0 else gathered[rows_at(dz, 1), cols]
            rows = jnp.dot(pick, tok, preferred_element_type=F32)
            cots = jnp.dot(pick_w, cot, preferred_element_type=F32)
            both = jnp.concatenate(
                [rows.reshape(plane, SLOTS, prep_tile), cots.reshape(plane, SLOTS, prep_tile)],
                axis=1,
            )
            sendb[first : first + plane, :, cols] = both.astype(BF)

    def push(place):
        first = place * plane
        chunk_sem = a2a_recv.at[first // block]
        pltpu.make_async_copy(sendb.at[first], recvb.at[first], chunk_sem).start()

        def send(j, carry):
            where = (replica(dp, j), shifted(me, j // GY, 0, j % GY))
            i = first + j
            remote(sendb.at[i], recvb.at[i], a2a_send, chunk_sem, where).start()
            return carry

        lax.fori_loop(1, plane, send, 0)

    for k in range(AHEAD):
        swap(k)
    hops = []
    if "D" in parts:
        meta[0] = jnp.zeros((SLOTS, tokens), F32)
        for k in range(3):
            code = route_ref[k : k + 1, :] * SLOTS + slot_ref[k : k + 1, :]
            meta[0, k : k + 1, :] = code.astype(F32)
            meta[0, 4 + k : 5 + k, :] = weight_ref[k : k + 1, :].astype(BF).astype(F32)
        for part, src in ((0, tok_ref), (1, cot_ref)):
            hop(src, 1, part, 1)
            hop(src, GZ - 1, part, -1)

        def send_meta(dz, carry):
            where = (dp, shifted(me, 0, dz, 0))
            remote(meta.at[0], meta.at[dz], meta_send, meta_recv, where).start()
            return carry

        lax.fori_loop(1, GZ, send_meta, 0)
        codes = codes_of(me, 0, picked, 0, flag_ref).astype(F32)
    lane = lax.broadcasted_iota(jnp.int32, flag_ref.shape, 1)
    mine = jnp.where(lane == me, flag_ref[...], 0).astype(F32)
    flagged = jnp.max(mine, axis=1, keepdims=True) > 0.5

    ff_tile = pick_tile(ff, 256)
    half_tile = pick_tile(half, 256)

    def forward_part(first, count):
        rows_n = count * SLOTS
        place = pl.ds(first * SLOTS, rows_n)
        for col in range(0, width, prep_tile):
            cols = slice(col, col + prep_tile)
            both = recvb[first : first + count, :, cols].astype(F32)
            rows_b[place, cols] = both[:, :SLOTS].reshape(rows_n, prep_tile).astype(BF)
            scaled_b[place, cols] = both[:, SLOTS:].reshape(rows_n, prep_tile).astype(BF)
        for f in range(0, 2 * ff, ff_tile):
            cols = slice(f, f + ff_tile)
            gate_up[:rows_n, cols] = jnp.dot(
                rows_b[place, :], full_g[:, cols], preferred_element_type=F32
            )

    def backward_part(first, count):
        rows_n = count * SLOTS
        place = pl.ds(first * SLOTS, rows_n)
        prob = jnp.zeros((rows_n, 1), F32)
        for f in range(0, ff, ff_tile):
            cols = slice(f, f + ff_tile)
            up_cols = slice(ff + f, ff + f + ff_tile)
            gate, up = gate_up[:rows_n, cols], gate_up[:rows_n, up_cols]
            hgrad = lax.dot_general(
                scaled_b[place, :], full_d[cols, :], ROWS_BY_ROWS, preferred_element_type=F32
            )
            sig = jax.nn.sigmoid(gate)
            silu = gate * sig
            hid = (silu * up).astype(BF)
            hid_b[place, cols] = hid
            both_b[place, cols] = (hgrad * up * sig * (1.0 + gate * (1.0 - sig))).astype(BF)
            both_b[place, up_cols] = (hgrad * silu).astype(BF)
            prob = prob + jnp.sum(hid.astype(F32) * hgrad, axis=1, keepdims=True)
        prob = jnp.broadcast_to(prob, (rows_n, LANES))
        rough = prob.astype(BF).astype(F32)
        both = jnp.concatenate(
            [rough.reshape(count, SLOTS, LANES), (prob - rough).reshape(count, SLOTS, LANES)],
            axis=1,
        )
        retb[first : first + count, :, half : half + LANES] = both.astype(BF)

    def row_grads(first, count):
        place = pl.ds(first * SLOTS, count * SLOTS)
        for col in range(0, half, half_tile):
            lo = lax.dot_general(
                both_b[place, :], full_g[col : col + half_tile, :], ROWS_BY_ROWS,
                preferred_element_type=F32,
            )
            hi = lax.dot_general(
                both_b[place, :], full_g[half + col : half + col + half_tile, :], ROWS_BY_ROWS,
                preferred_element_type=F32,
            )
            both = jnp.concatenate(
                [lo.reshape(count, SLOTS, half_tile), hi.reshape(count, SLOTS, half_tile)], axis=1
            )
            retb[first : first + count, :, col : col + half_tile] = both.astype(BF)

    def give_back(c):
        if "R" not in parts:
            return

        def send(j, carry):
            i = c * block + j

            @pl.when(i > 0)
            def _():
                remote(
                    retb.at[i], ret_ref.at[i], ret_send, ret_recv,
                    (replica(dp, i), partner(me, i, -1)),
                ).start()

            return carry

        lax.fori_loop(0, block, send, 0)

    def arrive(c):
        if "D" in parts:
            arrived = recvb.at[pl.ds(c * block, block)]
            pltpu.make_async_copy(arrived, arrived, a2a_recv.at[c]).wait()

    def weights(gathers, forwards):
        for k in gathers:
            if k < len(pieces):
                gather(k)
                swap(k + AHEAD)
        for k in forwards:
            if k < len(pieces):
                forward(k)

    total = PIECES_G + PIECES_D
    plan = {
        1: (range(FIRST), ()),
        2: (range(FIRST, total), range(FIRST)),
        3: ((), range(FIRST, total)),
    }
    if "D" in parts:
        prepare(0)
        if DEFER == 0:
            push(0)
        others = meta.at[pl.ds(1, GZ - 1)]
        pltpu.make_async_copy(others, others, meta_recv).wait()
    for t in range(1, GZ // 2):
        if "D" in parts:
            for part in range(2):
                landed(t, part)
                landed(GZ - t, part)
        if t <= DEFER:
            weights(*plan[t])
        if "D" in parts:
            for place in (2 * t - 1, 2 * t):
                prepare(place)
                if t > DEFER:
                    push(place)
            if t == DEFER:
                for place in range(2 * t + 1):
                    push(place)
        if t > DEFER:
            weights(*plan[t])
    if "D" in parts:
        for part in range(2):
            landed(GZ // 2, part)
        prepare(GZ - 1)
        push(GZ - 1)

    def complete(first, stop):
        for k in range(first, min(stop, len(pieces))):
            sibs[k].wait_recv()
            fwds[k].wait_recv()

    last = CHUNKS - 1
    ahead = last * block
    for c in range(last):
        arrive(c)
    complete(0, PIECES_G)
    if "C" in parts:
        forward_part(0, ahead)
    complete(PIECES_G, total)
    if "C" in parts:
        backward_part(0, ahead)
        row_grads(0, ahead)
    if "R" in parts:
        pltpu.make_async_copy(retb.at[0], ret_ref.at[0], ret_recv).start()
    for c in range(last):
        give_back(c)
    arrive(last)
    if "C" in parts:
        forward_part(ahead, block)
        backward_part(ahead, block)
        row_grads(ahead, block)
    give_back(last)

    wide = pick_tile(2 * ff, 768)
    d_tile = pick_tile(quarter_g, 256)

    def gate_up_grads(quarter, i):
        if "G" not in parts:
            return
        start = pl.multiple_of(quarter * quarter_g + i * d_tile, d_tile)
        left = rows_b[:, pl.ds(start, d_tile)]
        for c in range(0, 2 * ff, wide):
            part_g[pl.ds(start, d_tile), c : c + wide] = lax.dot_general(
                left, both_b[:, c : c + wide], COLS_BY_COLS, preferred_element_type=F32
            ).astype(BF)

    part_d = gathered

    def down_grads():
        for copy in hops:
            copy.wait_send()
        if "G" not in parts:
            return
        for f in range(0, ff, ff_tile):
            for c in range(0, width, prep_tile):
                part_d[f : f + ff_tile, c : c + prep_tile] = lax.dot_general(
                    hid_b[:, f : f + ff_tile], scaled_b[:, c : c + prep_tile], COLS_BY_COLS,
                    preferred_element_type=F32,
                ).astype(BF)

    def place_of(quarter, rows):
        return pl.ds(pl.multiple_of(quarter * rows, 16), rows)

    reds = []

    def to_sibling(slot, part, rows, landing, quarter, where, off, count):
        copy = remote(
            part.at[pl.ds(pl.multiple_of(quarter * rows + off, 16), count)],
            landing.at[where, pl.ds(off, count)],
            red_send.at[slot], red_recv.at[slot], (sib, me),
        )
        copy.start()
        reds.append(copy)

    outs = []

    def to_far(slot, part, rows, landing, out, off, count):
        reds[slot].wait_recv()
        mine = part[pl.ds(pl.multiple_of(far * rows + off, 16), count), :].astype(F32)
        place = pl.ds(off, count)
        landing[0, place, :] = (mine + landing[0, place, :].astype(F32)).astype(BF)
        copy = remote(
            landing.at[0, place], out.at[place], out_send.at[slot], out_recv.at[slot], (far, me)
        )
        copy.start()
        outs.append(copy)

    tiles = quarter_g // d_tile
    for i in range(tiles):
        gate_up_grads(far ^ 1, i)
        to_sibling(i, part_g, quarter_g, sib_g, far ^ 1, 0, i * d_tile, d_tile)
    for i in range(tiles):
        gate_up_grads(far, i)
        if i > 0:
            to_far(i - 1, part_g, quarter_g, sib_g, far_g, (i - 1) * d_tile, d_tile)
    to_far(tiles - 1, part_g, quarter_g, sib_g, far_g, (tiles - 1) * d_tile, d_tile)
    down_grads()
    to_sibling(tiles, part_d, quarter_d, sib_d, far ^ 1, 0, 0, quarter_d)
    to_sibling(tiles + 1, part_d, quarter_d, sib_d, dp ^ 1, 1, 0, quarter_d)
    for i in range(tiles):
        gate_up_grads(dp ^ 1, i)
    to_sibling(tiles + 2, part_g, quarter_g, sib_g, dp ^ 1, 1, 0, quarter_g)
    to_far(tiles, part_d, quarter_d, sib_d, far_d, 0, quarter_d)
    for i in range(tiles):
        gate_up_grads(dp, i)
    if "S" in parts:
        reds[tiles + 1].wait_recv()
        own_d[...] = (
            part_d[place_of(dp, quarter_d), :].astype(F32) + sib_d[1].astype(F32)
        ).astype(BF)
        reds[tiles + 2].wait_recv()
        own_g[...] = (
            part_g[place_of(dp, quarter_g), :].astype(F32) + sib_g[1].astype(F32)
        ).astype(BF)

    if "D" in parts:
        others = sendb.at[pl.ds(0, experts - GZ)]
        pltpu.make_async_copy(others, others, a2a_send).wait()
        others = meta.at[pl.ds(1, GZ - 1)]
        pltpu.make_async_copy(others, others, meta_send).wait()
    for copy in swaps + fars + sibs + fwds + reds:
        copy.wait_send()
    if "R" in parts:
        others = retb.at[pl.ds(1, experts - 1)]
        pltpu.make_async_copy(others, others, ret_send).wait()
        pltpu.make_async_copy(retb, retb, ret_recv).wait()
    for copy in outs:
        copy.wait()


def finish_kernel(
    ret_hbm, own_g, own_d, far_g, far_d, route_ref, slot_ref, weight_ref, flag_ref,
    tok_out, weight_out, out_g, out_d,
    ret_ref, a_g, b_g, a_d, b_d, sum_g, sum_d, tok_ref, in_sem, out_sem,
):
    experts, _, cols = ret_ref.shape
    half = cols - LANES
    rows = experts * SLOTS
    load_ret = pltpu.make_async_copy(ret_hbm, ret_ref, in_sem.at[0])
    load_ret.start()
    steps = 4
    step_g, step_d = a_g.shape[0] // steps, a_d.shape[0] // steps
    loads = []
    for k in range(steps):
        for n, (src, dst, step) in enumerate(
            ((own_g, a_g, step_g), (far_g, b_g, step_g), (own_d, a_d, step_d), (far_d, b_d, step_d))
        ):
            part = pl.ds(k * step, step)
            copy = pltpu.make_async_copy(src.at[part], dst.at[part], in_sem.at[1 + 4 * k + n])
            copy.start()
            loads.append(copy)
    codes = codes_of(lax.axis_index("expert"), 0, rows, 1, flag_ref)
    tokens = route_ref.shape[1]
    hits = []
    for k in range(3):
        code = (route_ref[k : k + 1, :] * SLOTS + slot_ref[k : k + 1, :]).astype(F32)
        hits.append(codes == jnp.broadcast_to(code, (LANES, tokens)).T[:, :1].astype(jnp.int32))
    pick = jnp.zeros(hits[0].shape, F32)
    for hit in hits:
        pick = jnp.where(hit, 1.0, pick)
    pick = pick.astype(BF)
    load_ret.wait()
    stores = []

    def store(src, dst, n):
        copy = pltpu.make_async_copy(src, dst, out_sem.at[n])
        copy.start()
        stores.append(copy)

    tile = pick_tile(half, 512)
    for c in range(0, half, tile):
        both = ret_ref[:, :, c : c + tile].astype(F32)
        lo = both[:, :SLOTS].reshape(rows, tile).astype(BF)
        hi = both[:, SLOTS:].reshape(rows, tile).astype(BF)
        tok_ref[:, c : c + tile] = jnp.dot(pick, lo, preferred_element_type=F32)
        tok_ref[:, half + c : half + c + tile] = jnp.dot(pick, hi, preferred_element_type=F32)
    store(tok_ref, tok_out, 0)
    for k in range(steps):
        for copy in loads[4 * k : 4 * k + 4]:
            copy.wait()
        part = pl.ds(k * step_g, step_g)
        sum_g[part, :] = a_g[part, :].astype(F32) + b_g[part, :].astype(F32)
        store(sum_g.at[part], out_g.at[part], 1 + 2 * k)
        part = pl.ds(k * step_d, step_d)
        sum_d[part, :] = a_d[part, :].astype(F32) + b_d[part, :].astype(F32)
        store(sum_d.at[part], out_d.at[part], 2 + 2 * k)
    both = ret_ref[:, :, half:].astype(F32)
    rough = both[:, :SLOTS].reshape(rows, LANES).astype(BF)
    rest = both[:, SLOTS:].reshape(rows, LANES).astype(BF)
    for k in range(3):
        one = jnp.where(hits[k], 1.0, 0.0).astype(BF)
        prob = jnp.dot(one, rough, preferred_element_type=F32)
        prob = prob + jnp.dot(one, rest, preferred_element_type=F32)
        weight_out[k : k + 1, :] = prob.T[:1, :] / weight_ref[k : k + 1, :].astype(BF).astype(F32)
    for copy in stores:
        copy.wait()


def body(parts, tokens, cotangent, routes, slot_index, route_weight, swap_flags, w_gate_up, w_down):
    tok_rows, width = tokens.shape
    experts = swap_flags.shape[0]
    ff = w_down.shape[1] * lax.axis_size("dp")
    rows = experts * SLOTS
    quarter_g, quarter_d = w_gate_up.shape[1], w_down.shape[1]
    pieces = PIECES_G + PIECES_D

    vmem = pl.BlockSpec(memory_space=pltpu.VMEM)
    hbm = pl.BlockSpec(memory_space=pl.ANY)
    dma = pltpu.SemaphoreType.DMA
    flops = 2 * rows * width * ff * 9
    ret, own_g, own_d, far_g, far_d = pl.pallas_call(
        functools.partial(exchange_kernel, parts, (experts, width, ff)),
        name="ex_" + "".join(parts),
        out_shape=(
            jax.ShapeDtypeStruct((experts, 2 * SLOTS, width // 2 + LANES), BF),
            jax.ShapeDtypeStruct((quarter_g, 2 * ff), BF),
            jax.ShapeDtypeStruct((quarter_d, width), BF),
            jax.ShapeDtypeStruct((quarter_g, 2 * ff), BF),
            jax.ShapeDtypeStruct((quarter_d, width), BF),
        ),
        in_specs=[vmem] * 8,
        out_specs=(hbm, vmem, vmem, hbm, hbm),
        scratch_shapes=[
            pltpu.VMEM((experts, 2 * SLOTS, width), BF),
            pltpu.VMEM((experts, 2 * SLOTS, width), BF),
            pltpu.VMEM((quarter_g, 2 * ff), BF),
            pltpu.VMEM((quarter_d, width), BF),
            pltpu.VMEM((width, 2 * ff), BF),
            pltpu.VMEM((ff, width), BF),
            pltpu.VMEM((rows, width), BF),
            pltpu.VMEM((rows, width), BF),
            pltpu.VMEM((rows, ff), BF),
            pltpu.VMEM((rows, 2 * ff), BF),
            pltpu.VMEM((experts, 2 * SLOTS, width // 2 + LANES), BF),
            pltpu.VMEM((width, 2 * ff), BF),
            pltpu.VMEM((2, quarter_g, 2 * ff), BF),
            pltpu.VMEM((2, quarter_d, width), BF),
            pltpu.VMEM((2 * (GZ - 1) * tok_rows, width), BF),
            pltpu.VMEM((GZ, SLOTS, tok_rows), F32),
            pltpu.VMEM((rows // CHUNKS * (CHUNKS - 1), 2 * ff), F32),
            dma((2 * GZ - 2,)), dma((2 * GZ - 2,)), dma, dma,
            dma, dma((CHUNKS,)), dma, dma,
            dma((pieces,)), dma((pieces,)), dma((pieces,)), dma((pieces,)),
            dma((pieces,)), dma((pieces,)), dma((pieces,)), dma((pieces,)),
            dma((8,)), dma((8,)), dma((4,)), dma((4,)),
        ],
        compiler_params=pltpu.CompilerParams(
            has_side_effects=True, vmem_limit_bytes=VMEM_BYTES
        ),
        cost_estimate=pl.CostEstimate(
            flops=flops, bytes_accessed=12 * 2**20, transcendentals=rows * ff
        ),
    )(
        routes.T, slot_index.T, route_weight.T, swap_flags[None], tokens, cotangent, w_gate_up[0], w_down[0]
    )

    grad_tokens, grad_weight, grad_gu, grad_dn = pl.pallas_call(
        finish_kernel,
        name="finish",
        out_shape=(
            jax.ShapeDtypeStruct((tok_rows, width), F32),
            jax.ShapeDtypeStruct((3, tok_rows), F32),
            jax.ShapeDtypeStruct((quarter_g, 2 * ff), F32),
            jax.ShapeDtypeStruct((quarter_d, width), F32),
        ),
        in_specs=[hbm] * 5 + [vmem] * 4,
        out_specs=(hbm, vmem, hbm, hbm),
        scratch_shapes=[
            pltpu.VMEM(ret.shape, BF),
            pltpu.VMEM((quarter_g, 2 * ff), BF),
            pltpu.VMEM((quarter_g, 2 * ff), BF),
            pltpu.VMEM((quarter_d, width), BF),
            pltpu.VMEM((quarter_d, width), BF),
            pltpu.VMEM((quarter_g, 2 * ff), F32),
            pltpu.VMEM((quarter_d, width), F32),
            pltpu.VMEM((tok_rows, width), F32),
            dma((17,)),
            dma((9,)),
        ],
        compiler_params=pltpu.CompilerParams(vmem_limit_bytes=VMEM_BYTES),
    )(
        ret, own_g, own_d, far_g, far_d,
        routes.T, slot_index.T, route_weight.T, swap_flags[None],
    )
    return (grad_tokens, grad_weight.T, grad_gu[None], grad_dn[None])


def solution(mesh):
    return jax.shard_map(
        functools.partial(body, 'DWCGRS'),
        mesh=mesh,
        in_specs=(
            P(("dp", "expert"), None),
            P(("dp", "expert"), None),
            P(("dp", "expert"), None),
            P(("dp", "expert"), None),
            P(("dp", "expert"), None),
            P(),
            P("expert", "dp", None),
            P("expert", "dp", None),
        ),
        out_specs=(
            P(("dp", "expert"), None),
            P(("dp", "expert"), None),
            P("expert", "dp", None),
            P("expert", "dp", None),
        ),
        check_vma=False,
    )
```
